512 devices in a mesh: ctx: 64 (over y, z), mp: 8 (over x, core).
Axes of the slice: x: 4, y: 4, z: 16, core: 2. Of those that a mesh axis runs over, the one named last changes fastest.
Arguments:
- residual: bfloat16 [16384, 2048], P('ctx', 'mp'), may hold values from -6 to 6
- delta_query: bfloat16 [16384, 2048], P('ctx', 'mp'), may hold values from -6 to 6
- delta_key: bfloat16 [16384, 2048], P('ctx', 'mp'), may hold values from -6 to 6
- delta_value: bfloat16 [16384, 4096], P('ctx', 'mp'), may hold values from -6 to 6
- write_strength: float32 [32, 16384], P('mp', 'ctx'), may hold values from 0.05 to 0.9
- log_decay: float32 [32, 16384], P('mp', 'ctx'), may hold values from -1 to 0
- output_gate: bfloat16 [16384, 4096], P('ctx', 'mp'), may hold values from -6 to 6
- norm_gain: float32 [128], replicated, may hold values from 0.1 to 1.9
- attn_query: bfloat16 [16384, 4096], P('ctx', 'mp'), may hold values from -9 to 9
- attn_key: bfloat16 [16384, 512], P('ctx'), may hold values from -9 to 9
- attn_value: bfloat16 [16384, 512], P('ctx'), may hold values from -6 to 6
- attn_gate: bfloat16 [16384, 4096], P('ctx', 'mp'), may hold values from -6 to 6
- positions: int32 [16384], P('ctx'), may hold values from 0 to 4095, as said below
- block_lists: int32 [128, 13], P('ctx'), may hold values from -1 to 127, as said below
- out_weight: bfloat16 [2, 4096, 2048], P(None, 'mp', 'ctx'), may hold values from -0.09375 to 0.09375
Outputs:
- mixed: bfloat16 [16384, 2048], P('ctx', 'mp')
The draws below stay inside these ranges and needn't reach their ends.
Inputs may be any that keep to these rules, and one draw needn't show every extreme that they name: `positions`: each entry is the token's offset from the first token of its document; documents follow one another. `block_lists`: row r starts with r itself, then distinct earlier blocks of the same shard of 256 tokens or of the 6 shards before it, then -1 for the unused entries; the number of used entries is ragged and some rows use all 13.
All inputs are finite; a program needn't handle non-finite values.
Results may differ from the reference program's by a relative error of at most 0.013.
Values may be sent and summed in bfloat16 or wider, within the bound.
A program may use at most 128 MiB of HBM per device.

```python
import math
import jax
import jax.numpy as jnp
from jax import lax

D = 2048
DELTA_HEADS = 32
HK = 16
DK = 128
DV = 128
AH = 16
KVH = 2
HA = 256
TOK_DEV = 256
BLK = 128
SPAN = 6
ROT = 64
SEQUENCE_TOKENS = 16384
BPD = 2
NQB = 128
MAXL = 13
NCAND = 14


def make_positions(key):
    seed_here = jax.random.fold_in(key, 11)
    longest = min(4096, SEQUENCE_TOKENS // 4)
    locations = jnp.arange(SEQUENCE_TOKENS, dtype=jnp.int32)
    starts = jax.random.randint(seed_here, (SEQUENCE_TOKENS,), 0, TOK_DEV) == 0
    starts = starts | (locations % longest == 0)
    starts = jnp.where(locations < longest, locations == 0, starts)
    marked = jnp.where(starts, locations, 0)
    begins = lax.cummax(marked, axis=0)
    return locations - begins


def make_attention(key):
    seed_query = jax.random.fold_in(key, 31)
    seed_key = jax.random.fold_in(key, 32)
    query_base = jnp.clip(jax.random.normal(seed_query, (SEQUENCE_TOKENS, AH, HA), jnp.float32), -6.0, 6.0)
    key_base = jnp.clip(jax.random.normal(seed_key, (SEQUENCE_TOKENS, KVH, HA), jnp.float32), -6.0, 6.0)
    return (query_base.reshape(SEQUENCE_TOKENS, AH * HA), key_base.reshape(SEQUENCE_TOKENS, KVH * HA))


def draw_attn_query(key, part):
    return make_attention(key)[0].astype(jnp.bfloat16)


def draw_attn_key(key, part):
    return make_attention(key)[1].astype(jnp.bfloat16)


def draw_positions(key, part):
    return make_positions(key)


def draw_delta_key(key, part):
    seed_scale = jax.random.fold_in(key, 41)
    seed_body = jax.random.fold_in(key, 42)
    scales = jnp.exp(jax.random.uniform(seed_scale, (HK, DK), jnp.float32, math.log(0.03), 0.0))
    body_part = jnp.clip(jax.random.normal(seed_body, (SEQUENCE_TOKENS, HK, DK), jnp.float32), -6.0, 6.0)
    return (body_part * scales).reshape(SEQUENCE_TOKENS, HK * DK).astype(jnp.bfloat16)


def draw_log_decay(key, part):
    random_keys = [jax.random.fold_in(key, 51 + number) for number in range(7)]
    share = 0.5
    quick = jax.random.uniform(random_keys[0], (DELTA_HEADS,), jnp.float32) < share
    quick_rate = jax.random.uniform(random_keys[1], (DELTA_HEADS,), jnp.float32, 1.0 / 50.0, 1.0 / 30.0)
    slow_rate = jnp.exp(jax.random.uniform(random_keys[2], (DELTA_HEADS,), jnp.float32, math.log(0.05), math.log(0.3))) / SEQUENCE_TOKENS
    decay_speed = jnp.where(quick, quick_rate, slow_rate)
    block_multiplier = jnp.exp(jax.random.uniform(random_keys[3], (DELTA_HEADS, SEQUENCE_TOKENS // BLK), jnp.float32, math.log(0.5), math.log(1.4)))
    block_multiplier = jnp.repeat(block_multiplier, BLK, axis=1)
    token_multiplier = jax.random.uniform(random_keys[4], (DELTA_HEADS, SEQUENCE_TOKENS), jnp.float32, 0.5, 1.5)
    cluster_position = jax.random.randint(random_keys[5], (DELTA_HEADS, 2), 0, SEQUENCE_TOKENS)
    cluster_depth = jax.random.uniform(random_keys[6], (DELTA_HEADS, 2), jnp.float32, math.log(1.25), math.log(2.0))
    locations = jnp.arange(SEQUENCE_TOKENS, dtype=jnp.int32)
    token_clusters = jnp.sum(jnp.where(locations[None, None, :] == cluster_position[:, :, None], cluster_depth[:, :, None], 0.0), 1)
    return -(decay_speed[:, None] * block_multiplier * token_multiplier) - token_clusters


def draw_block_lists(key, part):
    seed_here = jax.random.fold_in(key, 23)
    seed_cap = jax.random.fold_in(seed_here, 1)
    seed_heavy = jax.random.fold_in(seed_here, 2)
    seed_count = jax.random.fold_in(seed_here, 3)
    seed_score = jax.random.fold_in(seed_here, 4)
    block_index = jnp.arange(NQB, dtype=jnp.int32)
    owner = block_index // BPD
    shard_count = NQB // BPD
    lowest = jnp.maximum(0, (owner - SPAN) * BPD)
    earlier = block_index - lowest
    capacity = jax.random.randint(seed_cap, (shard_count,), 1, MAXL + 1)
    heavy = jax.random.randint(seed_heavy, (), SPAN, shard_count)
    capacity = capacity.at[heavy].set(MAXL)
    counts = jax.random.randint(seed_count, (NQB,), 0, 1 << 20) % capacity[owner] + 1
    counts = jnp.minimum(counts, earlier + 1)
    counts = jnp.where(block_index == heavy * BPD + BPD - 1, MAXL, counts)
    offsets = jnp.arange(1, NCAND, dtype=jnp.int32)
    scores = jax.random.randint(seed_score, (NQB, NCAND - 1), 0, 1 << 16) * 1024 + offsets[None, :]
    scores = jnp.where(offsets[None, :] <= earlier[:, None], scores, -1)
    _, picked = lax.top_k(scores, MAXL - 1)
    entries = block_index[:, None] - (picked + 1)
    slots = jnp.arange(1, MAXL, dtype=jnp.int32)
    entries = jnp.where(slots[None, :] < counts[:, None], entries, -1)
    return jnp.concatenate([block_index[:, None], entries], 1).astype(jnp.int32)


def level_of(stream_key, shape, pieces, least, top_value):
    loudness = 1.0
    for axis_at, blocks in pieces:
        heights = jax.random.uniform(jax.random.fold_in(jax.random.fold_in(stream_key, 6), axis_at), (blocks,), jnp.float32, least / len(pieces), top_value / len(pieces))
        loudness = loudness * jnp.repeat(jnp.exp(heights), shape[axis_at] // blocks).reshape((-1,) + (1,) * (len(shape) - 1 - axis_at))
    return loudness


def scatter_about(key, extent, deviation, limit, cuts=(), held_as=jnp.bfloat16):
    values = jax.random.normal(key, extent, jnp.float32) * deviation
    if len(cuts) > 0:
        values = level_of(key, extent, cuts, -0.22, 0.18) * values
    return jnp.clip(values, min=-limit, max=limit).astype(held_as)


def setup_inputs(seed: int = 0) -> dict:
    streams_of = jax.random.split(jax.random.key(seed), 16)
    return {
        "residual": scatter_about(streams_of[0], (SEQUENCE_TOKENS, D), 1.0, 6.0, ((0, 64), (1, 8))),
        "delta_query": scatter_about(streams_of[1], (SEQUENCE_TOKENS, HK * DK), 1.0, 6.0, ((0, 64), (1, 8))),
        "delta_key": draw_delta_key(jax.random.fold_in(streams_of[15], 71), 0),
        "delta_value": scatter_about(streams_of[3], (SEQUENCE_TOKENS, DELTA_HEADS * DV), 1.0, 6.0, ((0, 64), (1, 8))),
        "write_strength": jnp.clip(0.05 + 0.84999998 * jax.random.uniform(streams_of[4], (DELTA_HEADS, SEQUENCE_TOKENS), jnp.float32) ** level_of(streams_of[4], (DELTA_HEADS, SEQUENCE_TOKENS), ((0, 8), (1, 64)), -0.2, 0.2), 0.05, 0.9),
        "log_decay": draw_log_decay(jax.random.fold_in(streams_of[15], 71), 0),
        "output_gate": scatter_about(streams_of[6], (SEQUENCE_TOKENS, DELTA_HEADS * DV), 1.0, 6.0, ((0, 64), (1, 8))),
        "norm_gain": jnp.clip(1.0 + 0.18 * jax.random.normal(streams_of[7], (DV,), jnp.float32), 0.1, 1.9),
        "attn_query": draw_attn_query(jax.random.fold_in(streams_of[15], 71), 0),
        "attn_key": draw_attn_key(jax.random.fold_in(streams_of[15], 71), 0),
        "attn_value": scatter_about(streams_of[10], (SEQUENCE_TOKENS, KVH * HA), 1.0, 6.0, ((0, 64),)),
        "attn_gate": scatter_about(streams_of[11], (SEQUENCE_TOKENS, AH * HA), 1.0, 6.0, ((0, 64), (1, 8))),
        "positions": draw_positions(jax.random.fold_in(streams_of[15], 71), 0),
        "block_lists": draw_block_lists(jax.random.fold_in(streams_of[15], 71), 0),
        "out_weight": scatter_about(streams_of[14], (2, DELTA_HEADS * DV, D), (DELTA_HEADS * DV) ** -0.5, 0.09375, ((1, 8), (2, 64))),
    }


def unit_rows(matrix):
    return matrix * lax.rsqrt(lax.optimization_barrier(jnp.sum(matrix * matrix, -1, keepdims=True)) + 1e-06)

def rotate_rows(matrix, locations):
    half = ROT // 2
    freq = jnp.power(jnp.float32(10000000.0), -2.0 * jnp.arange(half, dtype=jnp.float32) / ROT)
    angle = locations.astype(jnp.float32)[..., None] * freq
    cosine = jnp.cos(angle)
    sine = jnp.sin(angle)
    first = matrix[..., :half]
    second = matrix[..., half:ROT]
    return jnp.concatenate([first * cosine - second * sine, second * cosine + first * sine, matrix[..., ROT:]], -1)

def reference(residual, delta_query, delta_key, delta_value, write_strength, log_decay, output_gate, norm_gain, attn_query, attn_key, attn_value, attn_gate, positions, block_lists, out_weight):
    exact_result = lax.Precision.HIGHEST
    share = DELTA_HEADS // HK
    unit_query = jnp.repeat(unit_rows(delta_query.astype(jnp.float32).reshape(SEQUENCE_TOKENS, HK, DK)), share, axis=1)
    unit_key = jnp.repeat(unit_rows(delta_key.astype(jnp.float32).reshape(SEQUENCE_TOKENS, HK, DK)), share, axis=1)
    value_rows = delta_value.astype(jnp.float32).reshape(SEQUENCE_TOKENS, DELTA_HEADS, DV)
    fade_rows = jnp.exp(log_decay).T
    write_rows = write_strength.T

    def advance(recurrent_state, inputs):
        current_query, current_key, value_now, fade_now, write_now = inputs
        recurrent_state = fade_now[:, None, None] * recurrent_state
        estimate = jnp.einsum('jn,jnl->jl', current_key, recurrent_state, precision=exact_result)
        recurrent_state = recurrent_state + current_key[:, :, None] * (write_now[:, None] * (value_now - estimate))[:, None, :]
        mixer_output = jnp.einsum('jn,jnl->jl', current_query, recurrent_state, precision=exact_result)
        return (recurrent_state, mixer_output)
    start = jnp.zeros((DELTA_HEADS, DK, DV), jnp.float32)
    _, delta_read = lax.scan(advance, start, (unit_query, unit_key, value_rows, fade_rows, write_rows))
    square_mean = lax.optimization_barrier(jnp.mean(delta_read * delta_read, -1, keepdims=True))
    gate_rows = jax.nn.silu(output_gate.astype(jnp.float32).reshape(SEQUENCE_TOKENS, DELTA_HEADS, DV))
    delta_mixed = (delta_read * lax.rsqrt(square_mean + 1e-06) * norm_gain * gate_rows).astype(jnp.bfloat16).reshape(SEQUENCE_TOKENS, DELTA_HEADS * DV)
    group_size = AH // KVH
    rotated_query = rotate_rows(attn_query.astype(jnp.float32).reshape(SEQUENCE_TOKENS, AH, HA), positions[:, None]).astype(jnp.bfloat16)
    rotated_key = rotate_rows(attn_key.astype(jnp.float32).reshape(SEQUENCE_TOKENS, KVH, HA), positions[:, None]).astype(jnp.bfloat16)
    query_blocks = rotated_query.reshape(NQB, BLK, KVH, group_size, HA)
    key_blocks = rotated_key.reshape(NQB, BLK, KVH, HA)
    value_blocks = attn_value.reshape(NQB, BLK, KVH, HA)
    scale = 1.0 / HA ** 0.5

    def attend(inputs):
        query_block, listing, block_index = inputs
        chosen = jnp.where(listing >= 0, listing, 0).astype(jnp.int32)
        keys_here = key_blocks[chosen].reshape(MAXL * BLK, KVH, HA).astype(jnp.float32)
        values_here = value_blocks[chosen].reshape(MAXL * BLK, KVH, HA).astype(jnp.float32)
        score = jnp.einsum('qgjd,kgd->gjqk', query_block.astype(jnp.float32), keys_here) * scale
        key_place = (chosen[:, None] * BLK + jnp.arange(BLK, dtype=jnp.int32)[None, :]).reshape(MAXL * BLK)
        key_live = jnp.repeat(listing >= 0, BLK)
        query_place = block_index * BLK + jnp.arange(BLK, dtype=jnp.int32)
        allowed = key_live[None, :] & (key_place[None, :] <= query_place[:, None])
        top = lax.optimization_barrier(jnp.max(jnp.where(allowed[None, None], score, -jnp.inf), -1, keepdims=True))
        weights = jnp.where(allowed[None, None], jnp.exp(score - top), 0.0)
        weights_bf16 = weights.astype(jnp.bfloat16)
        numer = jnp.einsum('gjqk,kgd->qgjd', weights_bf16.astype(jnp.float32), values_here).reshape(BLK, AH, HA)
        denom = lax.optimization_barrier(jnp.sum(weights, -1)).transpose(2, 0, 1).reshape(BLK, AH)
        return numer / denom[:, :, None]
    attn_read = lax.map(attend, (query_blocks, block_lists, jnp.arange(NQB, dtype=jnp.int32)))
    attn_read = attn_read.reshape(SEQUENCE_TOKENS, AH, HA)
    attn_mixed = (attn_read * jax.nn.sigmoid(attn_gate.astype(jnp.float32).reshape(SEQUENCE_TOKENS, AH, HA))).astype(jnp.bfloat16).reshape(SEQUENCE_TOKENS, AH * HA)
    total = residual.astype(jnp.float32) + jnp.dot(delta_mixed, out_weight[0], preferred_element_type=jnp.float32) + jnp.dot(attn_mixed, out_weight[1], preferred_element_type=jnp.float32)
    return total.astype(jnp.bfloat16)
```

```python
import functools

import jax
import jax.numpy as jnp
from jax import lax
from jax.experimental import pallas as pl
from jax.experimental.pallas import tpu as pltpu
from jax.sharding import PartitionSpec as P

DK = 128
AH = 16
KVH = 2
HA = 256
BLK = 128
SPAN = 6
ROT = 64
TOK = 256
ZN = 16
YN = 4
GRP = 4
MAPR = 144
LOGICAL = pl.DeviceIdType.MESH
F32 = jnp.float32
BF16 = jnp.bfloat16
VMEM = pl.BlockSpec(memory_space=pltpu.VMEM)
MB = 1 << 20


def dot(a, b):
    return jnp.dot(a, b, preferred_element_type=F32)


def dot_nt(a, b):
    return lax.dot_general(a, b, (((1,), (1,)), ((), ())), preferred_element_type=F32)


def split2(a):
    high = a.astype(BF16)
    return high, (a - high.astype(F32)).astype(BF16)


def dot3(a, b):
    ah, al = split2(a)
    bh, bl = split2(b)
    return dot(ah, bh) + (dot(ah, bl) + dot(al, bh))


def iota(shape, axis):
    return lax.broadcasted_iota(jnp.int32, shape, axis)


def block_inverse(lower):
    row = iota((TOK, 128), 0)
    lane = iota((TOK, 128), 1)
    left = jnp.where(row // 16 == lane // 16, lower[:, :128], 0.0)
    right = jnp.where(row // 16 == (lane + 128) // 16, lower[:, 128:], 0.0)
    folded = left + right
    for step in (64, 32, 16):
        folded = folded + pltpu.roll(folded, step, 1)
    low3 = folded.reshape(16, 16, 128)
    inv3 = jnp.where(row % 16 == lane % 16, 1.0, 0.0).astype(F32).reshape(16, 16, 128)
    for j in range(15):
        inv3 = inv3 - low3[:, :, j : j + 1] * inv3[:, j : j + 1, :]
    compact = inv3.reshape(TOK, 128)
    r1 = iota((128, 128), 0)
    c1 = iota((128, 128), 1)
    halves = []
    for part in range(2):
        rows = slice(part * 128, part * 128 + 128)
        inv = jnp.where(r1 // 16 == c1 // 16, compact[rows], 0.0)
        low = lower[rows, rows]
        for size in (16, 32, 64):
            between = (r1 // (2 * size) == c1 // (2 * size)) & (r1 // size != c1 // size)
            off = jnp.where(between, low, 0.0)
            inv = inv - dot3(inv, dot3(off, inv))
        halves.append(inv)
    cross = -dot3(halves[1], dot3(lower[128:, :128], halves[0]))
    top = jnp.concatenate([halves[0], jnp.zeros((128, 128), F32)], 1)
    return jnp.concatenate([top, jnp.concatenate([cross, halves[1]], 1)], 0)


def local_kernel(
    dq_ref, dk_ref, dv_ref, wr_ref, ld_ref, aq_ref, ak_ref, av_ref, turn_ref,
    maps_ref, r0_ref, qe_ref, qrot_ref, kv_ref,
):
    rr = iota((TOK, TOK), 0)
    cc = iota((TOK, TOK), 1)
    upto = rr >= cc
    strict = rr > cc
    diag = rr == cc
    decay = ld_ref[...]
    tri = jnp.where(rr <= cc, 1.0, 0.0).astype(F32)
    exact = lax.Precision.HIGHEST
    g_rows = jnp.dot(decay, tri, precision=exact, preferred_element_type=F32)
    g_cols = jnp.transpose(jnp.concatenate([g_rows, g_rows], 0))
    b_cols = jnp.transpose(jnp.concatenate([wr_ref[...], wr_ref[...]], 0))
    for kh in range(2):
        cols = slice(kh * DK, kh * DK + DK)
        kb = dk_ref[:, cols]
        qb = dq_ref[:, cols]
        qf = qb.astype(F32)
        gram = dot_nt(kb, kb)
        mixed = dot_nt(qb, kb)
        square = jnp.where(diag, gram, 0.0)
        rk_col = lax.rsqrt(jnp.sum(square, 1, keepdims=True) + 1e-06)
        rk_row = lax.rsqrt(jnp.sum(square, 0, keepdims=True) + 1e-06)
        rq_col = lax.rsqrt(jnp.sum(qf * qf, 1, keepdims=True) + 1e-06)
        kt = jnp.transpose(kb.astype(F32)).astype(BF16)
        for sub in range(2):
            h = kh * 2 + sub
            g_row = g_rows[h : h + 1]
            g_col = g_cols[:, h : h + 1]
            b_row = wr_ref[h : h + 1, :]
            b_col = b_cols[:, h : h + 1]
            fade = jnp.where(upto, jnp.exp(jnp.where(upto, g_col - g_row, 0.0)), 0.0)
            lower = jnp.where(strict, fade * gram, 0.0) * (b_col * rk_col) * rk_row
            inv = block_inverse(lower)
            vb = dv_ref[:, h * DK : h * DK + DK]
            th, tl = split2(inv * b_row)
            u = dot(th, vb) + dot(tl, vb)
            th, tl = split2(inv * (b_row * jnp.exp(g_row) * rk_row))
            w = dot(th, kb) + dot(tl, kb)
            both = jnp.concatenate([w, u], 1)
            g_end = g_col[TOK - 1 : TOK]
            pushed = (both * (jnp.exp(g_end - g_col) * rk_col)).astype(BF16)
            maps_ref[h, :DK, :] = dot(kt, pushed).astype(BF16)
            maps_ref[h, DK:, :] = gamma_rows(jnp.broadcast_to(jnp.exp(g_end), (1, 2 * DK)))
            reads = (fade * mixed * rq_col * rk_row).astype(BF16)
            seen = dot(reads, both.astype(BF16))
            r0_ref[h] = seen[:, DK:]
            qe_ref[h] = (jnp.exp(g_col) * rq_col * qf - seen[:, :DK]).astype(BF16)
    cosine = turn_ref[:, :128]
    sine = turn_ref[:, 128:]
    lane = iota((TOK, 128), 1)

    def rotate(x):
        swapped = jnp.where(lane < ROT // 2, pltpu.roll(x, 128 - ROT // 2, 1), pltpu.roll(x, ROT // 2, 1))
        return x * cosine + swapped * sine

    for head in range(2):
        rows = slice(head * TOK, head * TOK + TOK)
        first = aq_ref[:, head * HA : head * HA + 128].astype(F32)
        turned = rotate(first).astype(BF16)
        qrot_ref[rows, :128] = turned * BF16(1.0 / 16)
        qrot_ref[rows, 128:] = aq_ref[:, head * HA + 128 : head * HA + HA] * BF16(1.0 / 16)
    pair = lax.axis_index("mp") // 4
    keys = jnp.where(pair == 0, ak_ref[:, :HA], ak_ref[:, HA:])
    values = jnp.where(pair == 0, av_ref[:, :HA], av_ref[:, HA:])
    turned = rotate(keys[:, :128].astype(F32)).astype(BF16)
    for half in range(2):
        rows = slice(half * 128, half * 128 + 128)
        kv_ref[half, :128, :128] = turned[rows]
        kv_ref[half, :128, 128:] = keys[rows, 128:]
        kv_ref[half, 128:, :] = values[rows]


def gamma_rows(gamma):
    high = gamma.astype(BF16).astype(F32)
    middle = (gamma - high).astype(BF16).astype(F32)
    low = gamma - high - middle
    row = iota((16, gamma.shape[1]), 0)
    rows = jnp.where(row == 0, high, jnp.where(row == 1, middle, jnp.where(row == 2, low, 0.0)))
    return rows.astype(BF16)


def read_map(ref, index):
    tail = ref[index, DK:, :].astype(F32)
    gamma = tail[0:1] + tail[1:2] + tail[2:3]
    return gamma, ref[index, :DK, :].astype(F32)


def join(later, earlier):
    gl, xl = later
    ge, xe = earlier
    scaled = jnp.concatenate([xl[:, :DK] * ge[:, :DK], xl[:, DK:]], 1)
    return gl * ge, gl * xe + scaled - dot(xl[:, :DK].astype(BF16), xe.astype(BF16))


def apply_map(one, state):
    gamma, x = one
    return gamma[:, :DK] * state + x[:, DK:] - dot(x[:, :DK].astype(BF16), state.astype(BF16))


def write_map(ref, index, one):
    gamma, x = one
    ref[index, :DK, :] = x.astype(BF16)
    ref[index, DK:, :] = gamma_rows(gamma)


def chosen(index, options):
    result = options[0]
    for number in range(1, len(options)):
        result = jax.tree.map(lambda a, b: jnp.where(index == number, b, a), result, options[number])
    return result


def scan_kernel(
    maps_ref, qrot_ref, kv_ref, bias_ref, gate_ref,
    state_ref, attn_ref,
    l1, l2, l3, pre, pregam, ssend, sgot, kvbuf, m_scr, l_scr, acc,
    s1, r1, s2, r2, s3, r3, s4, r4, kzs, kzr, kcs, kcr,
):
    c = lax.axis_index("ctx")
    mp = lax.axis_index("mp")
    y = c // ZN
    z = c % ZN
    zlo = z % GRP
    zhi = z // GRP
    core = mp % 2
    sibling = mp + 1 - 2 * core
    after = (c + 1) % (ZN * YN)
    before = (c + ZN * YN - 1) % (ZN * YN)

    def lo_peer(d):
        return (zlo + d) % GRP

    def lo_dev(d):
        return (y * ZN + zhi * GRP + lo_peer(d), mp)

    def hi_dev(d):
        return (y * ZN + ((zhi + d) % GRP) * GRP + zlo, mp)

    def y_dev(d):
        return (((y + d) % YN) * ZN + z, mp)

    barrier = pltpu.get_barrier_semaphore()
    peers = [f(d) for f in (lo_dev, hi_dev, y_dev) for d in (1, 2, 3)]
    peers += [(after, mp), (before, mp), (c, sibling)]
    for peer in peers:
        pl.semaphore_signal(barrier, inc=1, device_id=peer, device_id_type=LOGICAL)
    pl.semaphore_wait(barrier, len(peers))

    def remote(src, dst, send, recv, device):
        return pltpu.make_async_remote_copy(
            src_ref=src, dst_ref=dst, send_sem=send, recv_sem=recv, device_id=device, device_id_type=LOGICAL
        )

    def c1(d):
        return remote(maps_ref.at[lo_peer(d)], l1.at[zlo], s1.at[d - 1], r1.at[d - 1], lo_dev(d))

    def c2(d):
        return remote(l2.at[zhi], l2.at[zhi], s2.at[d - 1], r2.at[d - 1], hi_dev(d))

    def c3(d):
        return remote(l3.at[y], l3.at[y], s3.at[d - 1], r3.at[d - 1], y_dev(d))

    def c4(d):
        return remote(ssend.at[lo_peer(d)], sgot.at[zlo], s4.at[d - 1], r4.at[d - 1], lo_dev(d))

    def kz(s):
        src = kv_ref.at[core] if s == 1 else kvbuf.at[s - 2, core]
        return remote(src, kvbuf.at[s - 1, core], kzs.at[s - 1], kzr.at[s - 1], (after, mp))

    def kc(s):
        return remote(kvbuf.at[s - 1, core], kvbuf.at[s - 1, core], kcs.at[s - 1], kcr.at[s - 1], (c, sibling))

    def kv_step(s):
        kz(s).wait_recv()
        if s < SPAN:
            kz(s + 1).start()
        kc(s).start()

    def attend(s):
        first = s == 0
        qk = []
        for half in range(2):
            keys = kv_ref[half, :128, :] if first else kvbuf[s - 1, half, :128, :]
            qk.append(dot_nt(qrot_ref[...], keys))
        score = jnp.concatenate(qk, 1)
        rows = bias_ref[2 * s : 2 * s + 2, :]
        bias = jnp.concatenate(
            [jnp.broadcast_to(rows[qb : qb + 1], (BLK, TOK)) for _ in range(2) for qb in range(2)], 0
        )
        score = score + bias
        if first:
            r = iota((2 * TOK, TOK), 0) % TOK
            score = jnp.where(iota((2 * TOK, TOK), 1) <= r, score, -1e30)
        top = jnp.max(score, 1, keepdims=True)
        if not first:
            old = m_scr[...]
            top = jnp.maximum(old, top)
            fade = jnp.exp(old - top)
        weights = jnp.exp(score - top)
        total = jnp.sum(weights, 1, keepdims=True)
        wb = weights.astype(BF16)
        part = None
        for half in range(2):
            values = kv_ref[half, 128:, :] if first else kvbuf[s - 1, half, 128:, :]
            term = dot(wb[:, half * 128 : half * 128 + 128], values)
            part = term if part is None else part + term
        m_scr[...] = top
        if first:
            l_scr[...] = total
            acc[...] = part
        else:
            l_scr[...] = l_scr[...] * fade + total
            acc[...] = acc[...] * fade + part

    for d in (2, 1, 3):
        c1(d).start()
    kz(1).start()
    l1[zlo] = maps_ref[zlo]
    attend(0)
    for d in (1, 2, 3):
        c1(d).wait_recv()
    run = read_map(l1, 0)
    for i in range(1, GRP):
        pre[i - 1] = run[1]
        pregam[i - 1] = run[0]
        run = join(read_map(l1, i), run)
    write_map(l2, zhi, run)
    for d in (2, 1, 3):
        c2(d).start()
    kv_step(1)
    kv_step(2)
    kc(1).wait_recv()
    attend(1)
    kv_step(3)
    kc(2).wait_recv()
    attend(2)
    for d in (1, 2, 3):
        c2(d).wait_recv()
    ones = jnp.ones((1, 2 * DK), F32)
    rps = [(ones, jnp.zeros((DK, 2 * DK), F32)), read_map(l2, 0)]
    for i in range(1, GRP):
        rps.append(join(read_map(l2, i), rps[-1]))
    write_map(l3, y, rps[GRP])
    for d in (2, 1, 3):
        c3(d).start()
    mine = chosen(zhi, rps[:GRP])
    kv_step(4)
    kc(3).wait_recv()
    attend(3)
    for d in (1, 2, 3):
        c3(d).wait_recv()
    carries = [jnp.zeros((DK, DK), F32), read_map(l3, 0)[1][:, DK:]]
    for i in range(1, YN - 1):
        carries.append(apply_map(read_map(l3, i), carries[-1]))
    carry = apply_map(mine, chosen(y, carries))
    ssend[0] = carry.astype(BF16)
    for i in range(1, GRP):
        ssend[i] = apply_map((pregam[i - 1], pre[i - 1]), carry).astype(BF16)
    for d in (2, 1, 3):
        c4(d).start()
    sgot[zlo] = ssend[zlo]
    kv_step(5)
    kc(4).wait_recv()
    attend(4)
    kv_step(6)
    kc(5).wait_recv()
    attend(5)
    kc(6).wait_recv()
    attend(6)
    for head in range(2):
        rows = slice(head * TOK, head * TOK + TOK)
        cols = slice(head * HA, head * HA + HA)
        gate = gate_ref[:, cols].astype(F32)
        read = acc[rows, :] / l_scr[rows, :]
        attn_ref[:, cols] = (read / (1.0 + jnp.exp(-gate))).astype(BF16)
    for d in (1, 2, 3):
        c4(d).wait_recv()
    state_ref[...] = sgot[...]
    for d in (1, 2, 3):
        c1(d).wait_send()
        c2(d).wait_send()
        c3(d).wait_send()
        c4(d).wait_send()
    for s in range(1, SPAN + 1):
        kz(s).wait_send()
        kc(s).wait_send()


def final_kernel(
    state_ref, r0_ref, qe_ref, gate_ref, gain_ref, attn_ref, weight_ref,
    out_ref,
    mixed, sbuf, rbuf, ss, rs,
):
    c = lax.axis_index("ctx")
    mp = lax.axis_index("mp")

    def dev(d):
        return (c, (mp + d) % 8)

    barrier = pltpu.get_barrier_semaphore()
    for d in range(1, 8):
        pl.semaphore_signal(barrier, inc=1, device_id=dev(d), device_id_type=LOGICAL)
    for h in range(4):
        cols = slice(h * DK, h * DK + DK)
        read = r0_ref[h] + dot(qe_ref[h], state_ref[h])
        scale = lax.rsqrt(jnp.mean(read * read, 1, keepdims=True) + 1e-06)
        gate = gate_ref[:, cols].astype(F32)
        silu = gate / (1.0 + jnp.exp(-gate))
        mixed[:, cols] = (read * scale * gain_ref[...] * silu).astype(BF16)
    pl.semaphore_wait(barrier, 7)

    def copy(d):
        return pltpu.make_async_remote_copy(
            src_ref=sbuf.at[d - 1],
            dst_ref=rbuf.at[d - 1],
            send_sem=ss.at[d - 1],
            recv_sem=rs.at[d - 1],
            device_id=dev(d),
            device_id_type=LOGICAL,
        )

    def term(d):
        to = (mp + d) % 8
        first = weight_ref[to, :, 0].reshape(256, 512)
        second = weight_ref[to, :, 1].reshape(256, 512)
        return (dot_nt(mixed[...], first) + dot_nt(attn_ref[...], second)).astype(BF16)

    for d in (4, 3, 5, 2, 6, 1, 7):
        sbuf[d - 1] = term(d)
        copy(d).start()
    total = term(0).astype(F32)
    for d in (4, 3, 5, 2, 6, 1, 7):
        copy(d).wait_recv()
        total = total + rbuf[d - 1].astype(F32)
    out_ref[...] = total
    for d in range(1, 8):
        copy(d).wait_send()


def per_device(
    residual,
    delta_query,
    delta_key,
    delta_value,
    write_strength,
    log_decay,
    output_gate,
    norm_gain,
    attn_query,
    attn_key,
    attn_value,
    attn_gate,
    positions,
    block_lists,
    out_weight,
):
    weight_rows = jnp.transpose(out_weight, (2, 0, 1))
    weight_all = lax.all_gather(weight_rows, "ctx", axis=0, tiled=True)
    weight_all = weight_all.reshape(8, 8, 32, 2, 512).transpose(0, 1, 3, 2, 4)

    half = ROT // 2
    freq = jnp.power(jnp.float32(10000000.0), -2.0 * jnp.arange(half, dtype=F32) / ROT)
    angle = positions.astype(F32)[:, None] * freq
    cosine = jnp.cos(angle)
    sine = jnp.sin(angle)
    ones = jnp.ones((TOK, 128 - ROT), F32)
    turn = jnp.concatenate([cosine, cosine, ones, -sine, sine, 0 * ones], 1)

    here = lax.axis_index("ctx")
    candidates = (here[None] - jnp.arange(SPAN + 1, dtype=jnp.int32))[:, None] * 2 + jnp.arange(2, dtype=jnp.int32)
    listed = jnp.any(block_lists[None, :, None, :] == candidates[:, None, :, None], -1)
    listed = listed & (candidates >= 0)[:, None, :]
    bias = jnp.where(listed, 0.0, -1e30).astype(F32)
    bias = jnp.repeat(bias, BLK, axis=2).reshape(2 * (SPAN + 1), TOK)
    bias = jnp.concatenate([bias, jnp.zeros((2, TOK), F32)], 0)

    shape = jax.ShapeDtypeStruct
    maps, r0, qe, qrot, kv = pl.pallas_call(
        local_kernel,
        out_shape=(
            shape((4, MAPR, 2 * DK), BF16),
            shape((4, TOK, DK), F32),
            shape((4, TOK, DK), BF16),
            shape((2 * TOK, HA), BF16),
            shape((2, TOK, HA), BF16),
        ),
        in_specs=[VMEM] * 9,
        out_specs=(VMEM,) * 5,
        compiler_params=pltpu.CompilerParams(vmem_limit_bytes=48 * MB),
        cost_estimate=pl.CostEstimate(flops=2 * 10**9, bytes_accessed=4 * 10**6, transcendentals=10**6),
        name="delta_local",
    )(delta_query, delta_key, delta_value, write_strength, log_decay, attn_query, attn_key, attn_value, turn)

    dma = pltpu.SemaphoreType.DMA
    state, attn_mixed = pl.pallas_call(
        scan_kernel,
        out_shape=(shape((4, DK, DK), BF16), shape((TOK, 2 * HA), BF16)),
        in_specs=[VMEM] * 5,
        out_specs=(VMEM,) * 2,
        scratch_shapes=[
            pltpu.VMEM((GRP, MAPR, 2 * DK), BF16),
            pltpu.VMEM((GRP, MAPR, 2 * DK), BF16),
            pltpu.VMEM((YN, MAPR, 2 * DK), BF16),
            pltpu.VMEM((GRP - 1, DK, 2 * DK), F32),
            pltpu.VMEM((GRP - 1, 1, 2 * DK), F32),
            pltpu.VMEM((GRP, DK, DK), BF16),
            pltpu.VMEM((GRP, DK, DK), BF16),
            pltpu.VMEM((SPAN, 2, TOK, HA), BF16),
            pltpu.VMEM((2 * TOK, 1), F32),
            pltpu.VMEM((2 * TOK, 1), F32),
            pltpu.VMEM((2 * TOK, HA), F32),
        ]
        + [dma((3,))] * 8
        + [dma((SPAN,))] * 4,
        compiler_params=pltpu.CompilerParams(
            vmem_limit_bytes=48 * MB, collective_id=1, has_side_effects=True
        ),
        cost_estimate=pl.CostEstimate(flops=2 * 10**9, bytes_accessed=10**8, transcendentals=10**6),
        name="scan_attend",
    )(maps, qrot, kv, bias, attn_gate)

    summed = pl.pallas_call(
        final_kernel,
        out_shape=shape((TOK, 256), F32),
        in_specs=[VMEM] * 7,
        out_specs=VMEM,
        scratch_shapes=[
            pltpu.VMEM((TOK, 4 * DK), BF16),
            pltpu.VMEM((7, TOK, 256), BF16),
            pltpu.VMEM((7, TOK, 256), BF16),
            dma((7,)),
            dma((7,)),
        ],
        compiler_params=pltpu.CompilerParams(
            vmem_limit_bytes=48 * MB, collective_id=2, has_side_effects=True
        ),
        name="project_sum",
    )(state, r0, qe, output_gate, norm_gain.reshape(1, DK), attn_mixed, weight_all)
    return (residual.astype(F32) + summed).astype(BF16)


def solution(mesh):
    return jax.shard_map(
        per_device,
        mesh=mesh,
        in_specs=(
            P("ctx", "mp"),
            P("ctx", "mp"),
            P("ctx", "mp"),
            P("ctx", "mp"),
            P("mp", "ctx"),
            P("mp", "ctx"),
            P("ctx", "mp"),
            P(),
            P("ctx", "mp"),
            P("ctx", None),
            P("ctx", None),
            P("ctx", "mp"),
            P("ctx"),
            P("ctx", None),
            P(None, "mp", "ctx"),
        ),
        out_specs=P("ctx", "mp"),
        check_vma=False,
    )
```

```python
import jax
import jax.numpy as jnp
import numpy as np
from jax import lax
from jax.experimental import pallas as pl
from jax.experimental.pallas import tpu as pltpu
from jax.sharding import PartitionSpec as P

DK = 128
AH = 16
KVH = 2
HA = 256
BLK = 128
SPAN = 6
ROT = 64
TOK = 256
ZN = 16
YN = 4
GRP = 4
MAPR = 144
MESH = pl.DeviceIdType.MESH
F32 = jnp.float32
BF16 = jnp.bfloat16
ANY = pl.BlockSpec(memory_space=pl.ANY)
VMEM = pl.BlockSpec(memory_space=pltpu.VMEM)
MB = 1 << 20


def dot(a, b):
    return jnp.dot(a, b, preferred_element_type=F32)


def dot_nt(a, b):
    return lax.dot_general(a, b, (((1,), (1,)), ((), ())), preferred_element_type=F32)


def iota(shape, axis):
    return lax.broadcasted_iota(jnp.int32, shape, axis)


def base_inverse(lower):
    row = iota((TOK, 128), 0)
    lane = iota((TOK, 128), 1)
    left = jnp.where(row // 16 == lane // 16, lower[:, :128], 0.0)
    right = jnp.where(row // 16 == (lane + 128) // 16, lower[:, 128:], 0.0)
    folded = left + right
    for step in (64, 32, 16):
        folded = folded + pltpu.roll(folded, step, 1)
    low3 = folded.reshape(16, 16, 128)
    inv3 = jnp.where(row % 16 == lane % 16, 1.0, 0.0).astype(F32).reshape(16, 16, 128)
    for j in range(15):
        inv3 = inv3 - low3[:, :, j : j + 1] * inv3[:, j : j + 1, :]
    return inv3.reshape(TOK, 128)


def merge_blocks(lower, compact):
    r1 = iota((128, 128), 0)
    c1 = iota((128, 128), 1)
    halves = []
    for part in range(2):
        rows = slice(part * 128, part * 128 + 128)
        inv = jnp.where(r1 // 16 == c1 // 16, compact[rows], 0.0)
        low = lower[rows, rows]
        for size in (16, 32, 64):
            between = (r1 // (2 * size) == c1 // (2 * size)) & (r1 // size != c1 // size)
            off = jnp.where(between, low, 0.0)
            hi = inv.astype(BF16)
            inv = inv - dot(hi, dot(off.astype(BF16), hi).astype(BF16))
        halves.append(inv)
    inner = dot(lower[128:, :128].astype(BF16), halves[0].astype(BF16))
    cross = -dot(halves[1].astype(BF16), inner.astype(BF16))
    top = jnp.concatenate([halves[0], jnp.zeros((128, 128), F32)], 1)
    return jnp.concatenate([top, jnp.concatenate([cross, halves[1]], 1)], 0)


def gamma_rows(gamma):
    high = gamma.astype(BF16).astype(F32)
    middle = (gamma - high).astype(BF16).astype(F32)
    low = gamma - high - middle
    row = iota((16, gamma.shape[1]), 0)
    rows = jnp.where(row == 0, high, jnp.where(row == 1, middle, jnp.where(row == 2, low, 0.0)))
    return rows.astype(BF16)


def read_map(ref, index):
    tail = ref[index, DK:, :].astype(F32)
    gamma = tail[0:1] + tail[1:2] + tail[2:3]
    return gamma, ref[index, :DK, :].astype(F32)


def join(later, earlier):
    gl, xl = later
    ge, xe = earlier
    scaled = jnp.concatenate([xl[:, :DK] * ge[:, :DK], xl[:, DK:]], 1)
    return gl * ge, gl * xe + scaled - dot(xl[:, :DK].astype(BF16), xe.astype(BF16))


def apply_map(one, state):
    gamma, x = one
    return gamma[:, :DK] * state + x[:, DK:] - dot(x[:, :DK].astype(BF16), state.astype(BF16))


def write_map(ref, index, one):
    gamma, x = one
    ref[index, :DK, :] = x.astype(BF16)
    ref[index, DK:, :] = gamma_rows(gamma)


def mixer_kernel(
    w_hbm, dk_hbm, dq_hbm, dv_hbm, ak_hbm, av_hbm, aq_hbm, og_hbm, ag_hbm,
    wr_ref, ld_ref, pos_ref, list_ref, turn_ref, gain_ref,
    out_ref,
    wall, dk_ref, dq_ref, dv_ref, ak_ref, av_ref, aq_ref, og_ref, ag_ref,
    low_s, both_s, reads_s, r0_s, qe_s, qrot, own,
    maps, l1, l2, l3, pre, pregam, prefix, prefgam, csend, cgot, ssend, sgot,
    kvbuf, m_scr, l_scr, acc, mixed, attn, sbuf, rbuf,
    ins, s1, r1, s2, r2, s3, r3, sc, rc, s4, r4, kzs, kzr, kcs, kcr, wps, wpr, wms, wmr, wys, wyr, rss, rsr,
):
    c = lax.axis_index("ctx")
    mp = lax.axis_index("mp")
    y = c // ZN
    z = c % ZN
    zlo = z % GRP
    zhi = z // GRP
    core = mp % 2
    sibling = mp + 1 - 2 * core
    after = (c + 1) % (ZN * YN)
    before = (c + ZN * YN - 1) % (ZN * YN)
    z_up = (y * ZN + (z + 1) % ZN, mp)
    z_down = (y * ZN + (z + ZN - 1) % ZN, mp)

    def lo_peer(d):
        return (zlo + d) % GRP

    def lo_dev(d):
        return (y * ZN + zhi * GRP + lo_peer(d), mp)

    def hi_dev(d):
        return (y * ZN + ((zhi + d) % GRP) * GRP + zlo, mp)

    def y_dev(d):
        return (((y + d) % YN) * ZN + z, mp)

    def mp_dev(d):
        return (c, (mp + d) % 8)

    barrier = pltpu.get_barrier_semaphore()
    peers = [f(d) for f in (lo_dev, hi_dev, y_dev) for d in (1, 2, 3)] + [mp_dev(d) for d in range(1, 8)]
    peers += [(after, mp), (before, mp), z_up, z_down]
    for peer in peers:
        pl.semaphore_signal(barrier, inc=1, device_id=peer, device_id_type=MESH)

    moves = [
        (w_hbm, wall.at[y, z]),
        (dk_hbm, dk_ref),
        (dq_hbm, dq_ref),
        (ak_hbm, ak_ref),
        (av_hbm, av_ref),
        (dv_hbm, dv_ref),
        (aq_hbm, aq_ref),
        (ag_hbm, ag_ref),
        (og_hbm, og_ref),
    ]
    moves = [pltpu.make_async_copy(src, dst, ins.at[i]) for i, (src, dst) in enumerate(moves)]
    for move in moves:
        move.start()

    def remote(src, dst, send, recv, device):
        return pltpu.make_async_remote_copy(
            src_ref=src, dst_ref=dst, send_sem=send, recv_sem=recv, device_id=device, device_id_type=MESH
        )

    def c1(d):
        return remote(maps.at[lo_peer(d)], l1.at[zlo], s1.at[d - 1], r1.at[d - 1], lo_dev(d))

    def c2(d):
        return remote(l2.at[zhi], l2.at[zhi], s2.at[d - 1], r2.at[d - 1], hi_dev(d))

    def c3(d):
        return remote(l3.at[y], l3.at[y], s3.at[d - 1], r3.at[d - 1], y_dev(d))

    def cc(d):
        return remote(csend, cgot, sc.at[d - 1], rc, hi_dev(d))

    def c4(d):
        return remote(ssend.at[lo_peer(d)], sgot.at[zlo], s4.at[d - 1], r4.at[d - 1], lo_dev(d))

    def kz(s):
        src = own.at[core] if s == 1 else kvbuf.at[s - 2, core]
        return remote(src, kvbuf.at[s - 1, core], kzs.at[s - 1], kzr.at[s - 1], (after, mp))

    def kc(s):
        return remote(kvbuf.at[s - 1, core], kvbuf.at[s - 1, core], kcs.at[s - 1], kcr.at[s - 1], (c, sibling))

    def kv_step(s):
        kz(s).wait_recv()
        if s < SPAN:
            kz(s + 1).start()
        kc(s).start()

    def wz_up(k):
        block = wall.at[y, (z + ZN - k + 1) % ZN]
        return remote(block, block, wps.at[k - 1], wpr.at[k - 1], z_up)

    def wz_down(k):
        block = wall.at[y, (z + k - 1) % ZN]
        return remote(block, block, wms.at[k - 1], wmr.at[k - 1], z_down)

    def wy_send(zs):
        for d in (2, 1, 3):
            remote(wall.at[y, zs], wall.at[y, zs], wys.at[d - 1], wyr.at[d - 1], y_dev(d)).start()

    def wy_all(d):
        return remote(wall.at[y], wall.at[y], wys.at[d - 1], wyr.at[d - 1], y_dev(d))

    up_steps, down_steps = ZN // 2, ZN // 2 - 1

    def w_step(k):
        wz_up(k).wait_recv()
        if k < up_steps:
            wz_up(k + 1).start()
        if k <= down_steps:
            wz_down(k).wait_recv()
            if k < down_steps:
                wz_down(k + 1).start()
        wy_send((z + ZN - k) % ZN)
        if k <= down_steps:
            wy_send((z + k) % ZN)

    rr = iota((TOK, TOK), 0)
    cc2 = iota((TOK, TOK), 1)
    upto = rr >= cc2
    strict = rr > cc2
    diag = rr == cc2
    tri = jnp.where(rr <= cc2, 1.0, 0.0).astype(F32)
    exact = lax.Precision.HIGHEST
    g_rows = jnp.dot(ld_ref[...], tri, precision=exact, preferred_element_type=F32)
    g_cols = jnp.transpose(jnp.concatenate([g_rows, g_rows], 0))
    b_cols = jnp.transpose(jnp.concatenate([wr_ref[...], wr_ref[...]], 0))
    place = jnp.transpose(jnp.broadcast_to(pos_ref[...].astype(F32), (8, TOK)))[:, 0:1]
    angle = place * turn_ref[0:1, :]
    cosine = jnp.cos(angle)
    sine = jnp.sin(angle) * turn_ref[1:2, :]
    lane = iota((TOK, 128), 1)

    def rotate(x):
        swapped = jnp.where(lane < ROT // 2, pltpu.roll(x, 128 - ROT // 2, 1), pltpu.roll(x, ROT // 2, 1))
        return x * cosine + swapped * sine

    moves[1].wait()
    moves[2].wait()
    rk_cols = []
    rq_cols = []
    rk_rows = []
    for kh in range(2):
        cols = slice(kh * DK, kh * DK + DK)
        kb = dk_ref[:, cols]
        qb = dq_ref[:, cols]
        qf = qb.astype(F32)
        gram = dot_nt(kb, kb)
        cross = dot_nt(qb, kb)
        square = jnp.where(diag, gram, 0.0)
        rk_col = lax.rsqrt(jnp.sum(square, 1, keepdims=True) + 1e-06)
        rk_row = lax.rsqrt(jnp.sum(square, 0, keepdims=True) + 1e-06)
        rq_col = lax.rsqrt(jnp.sum(qf * qf, 1, keepdims=True) + 1e-06)
        rk_cols.append(rk_col)
        rk_rows.append(rk_row)
        rq_cols.append(rq_col)
        for h in (2 * kh, 2 * kh + 1):
            spread = g_cols[:, h : h + 1] - g_rows[h : h + 1]
            fade = jnp.where(upto, jnp.exp(jnp.where(upto, spread, 0.0)), 0.0)
            low_s[h] = jnp.where(strict, fade * gram, 0.0) * (b_cols[:, h : h + 1] * rk_col) * rk_row
            reads_s[h] = (fade * cross * rq_col * rk_row).astype(BF16)

    moves[0].wait()
    pl.semaphore_wait(barrier, len(peers))
    wz_up(1).start()
    wz_down(1).start()
    wy_send(z)

    moves[3].wait()
    moves[4].wait()
    pair = mp // 4
    keys = jnp.where(pair == 0, ak_ref[:, :HA], ak_ref[:, HA:])
    values = jnp.where(pair == 0, av_ref[:, :HA], av_ref[:, HA:])
    turned = rotate(keys[:, :128].astype(F32)).astype(BF16)
    for half in range(2):
        rows = slice(half * 128, half * 128 + 128)
        own[half, :128, :128] = turned[rows]
        own[half, :128, 128:] = keys[rows, 128:]
        own[half, 128:, :] = values[rows]
    kz(1).start()

    bases = [base_inverse(low_s[h]) for h in range(4)]
    w_step(1)
    inverses = [merge_blocks(low_s[h], bases[h]) for h in range(4)]
    w_step(2)
    moves[5].wait()
    for h in range(4):
        kb = dk_ref[:, (h // 2) * DK : (h // 2) * DK + DK]
        kt = jnp.transpose(kb.astype(F32)).astype(BF16)
        g_row = g_rows[h : h + 1]
        g_col = g_cols[:, h : h + 1]
        b_row = wr_ref[h : h + 1, :]
        u = dot((inverses[h] * b_row).astype(BF16), dv_ref[:, h * DK : h * DK + DK])
        w = dot((inverses[h] * (b_row * jnp.exp(g_row) * rk_rows[h // 2])).astype(BF16), kb)
        both = jnp.concatenate([w, u], 1)
        both_s[h] = both.astype(BF16)
        g_end = g_col[TOK - 1 : TOK]
        pushed = (both * (jnp.exp(g_end - g_col) * rk_cols[h // 2])).astype(BF16)
        maps[h, :DK, :] = dot(kt, pushed).astype(BF16)
        maps[h, DK:, :] = gamma_rows(jnp.broadcast_to(jnp.exp(g_end), (1, 2 * DK)))
    for d in (2, 1, 3):
        c1(d).start()
    l1[zlo] = maps[zlo]
    w_step(3)

    for h in range(4):
        cols = slice((h // 2) * DK, (h // 2) * DK + DK)
        seen = dot(reads_s[h], both_s[h])
        r0_s[h] = seen[:, DK:]
        qf = dq_ref[:, cols].astype(F32)
        qe_s[h] = (jnp.exp(g_cols[:, h : h + 1]) * rq_cols[h // 2] * qf - seen[:, :DK]).astype(BF16)
    moves[6].wait()
    for head in range(2):
        rows = slice(head * TOK, head * TOK + TOK)
        first = aq_ref[:, head * HA : head * HA + 128].astype(F32)
        qrot[rows, :128] = rotate(first).astype(BF16) * BF16(1.0 / 16)
        qrot[rows, 128:] = aq_ref[:, head * HA + 128 : head * HA + HA] * BF16(1.0 / 16)
    kv_step(1)
    w_step(4)

    entries = list_ref[...]
    row16 = iota((16, TOK), 0)
    candidate = (c - row16 // 2) * 2 + iota((16, TOK), 1) // BLK
    hit = jnp.zeros((16, TOK), F32)
    for e in range(entries.shape[1]):
        entry = jnp.where(row16 % 2 == 0, entries[0:1, e : e + 1], entries[1:2, e : e + 1])
        hit = jnp.where(candidate == entry, 1.0, hit)
    bias16 = jnp.where((hit > 0.5) & (candidate >= 0), 0.0, -1e30)

    def attend(s):
        first = s == 0
        qk = []
        for half in range(2):
            block = own[half, :128, :] if first else kvbuf[s - 1, half, :128, :]
            qk.append(dot_nt(qrot[...], block))
        score = jnp.concatenate(qk, 1)
        rows = bias16[2 * s : 2 * s + 2, :]
        bias = jnp.concatenate(
            [jnp.broadcast_to(rows[qb : qb + 1], (BLK, TOK)) for _ in range(2) for qb in range(2)], 0
        )
        score = score + bias
        if first:
            r = iota((2 * TOK, TOK), 0) % TOK
            score = jnp.where(iota((2 * TOK, TOK), 1) <= r, score, -1e30)
        top = jnp.max(score, 1, keepdims=True)
        if not first:
            old = m_scr[...]
            top = jnp.maximum(old, top)
            fade = jnp.exp(old - top)
        weights = jnp.exp(score - top)
        total = jnp.sum(weights, 1, keepdims=True)
        wb = weights.astype(BF16)
        part = None
        for half in range(2):
            block = own[half, 128:, :] if first else kvbuf[s - 1, half, 128:, :]
            term = dot(wb[:, half * 128 : half * 128 + 128], block)
            part = term if part is None else part + term
        m_scr[...] = top
        if first:
            l_scr[...] = total
            acc[...] = part
        else:
            l_scr[...] = l_scr[...] * fade + total
            acc[...] = acc[...] * fade + part

    attend(0)
    for d in (1, 2, 3):
        c1(d).wait_recv()
    run = read_map(l1, 0)
    for i in range(1, GRP):
        pre[i - 1] = run[1]
        pregam[i - 1] = run[0]
        run = join(read_map(l1, i), run)
    write_map(l2, zhi, run)
    for d in (1, 2, 3):

        @pl.when(zhi + d < GRP)
        def _():
            c2(d).start()

    kv_step(2)
    w_step(5)
    kc(1).wait_recv()
    attend(1)
    w_step(6)

    for d in (1, 2, 3):

        @pl.when(zhi >= d)
        def _():
            c2(d).wait_recv()

    for number in range(1, GRP):

        @pl.when(zhi == number)
        def _():
            run = read_map(l2, 0)
            for i in range(1, number):
                run = join(read_map(l2, i), run)
            prefgam[...] = run[0]
            prefix[...] = run[1]

    last = zhi == GRP - 1

    @pl.when(last)
    def _():
        total = join(read_map(l2, GRP - 1), (prefgam[...], prefix[...]))
        write_map(l3, y, total)
        for d in (2, 1, 3):
            c3(d).start()

    kv_step(3)
    w_step(7)
    kc(2).wait_recv()
    attend(2)

    @pl.when(last)
    def _():
        for d in (1, 2, 3):
            c3(d).wait_recv()
        state = jnp.zeros((DK, DK), F32)
        carry = state
        for i in range(YN - 1):
            state = apply_map(read_map(l3, i), state)
            carry = jnp.where(y == i + 1, state, carry)
        csend[...] = carry.astype(BF16)
        for d in (2, 1, 3):
            cc(d).start()

    kv_step(4)
    w_step(8)
    kc(3).wait_recv()

    @pl.when(jnp.logical_not(last))
    def _():
        attend(3)
        remote(csend, cgot, sc.at[0], rc, hi_dev(1)).wait_recv()

    @pl.when(last)
    def _():
        cgot[...] = csend[...]

    ssend[0] = cgot[...]

    @pl.when(zhi > 0)
    def _():
        ssend[0] = apply_map((prefgam[...], prefix[...]), cgot[...].astype(F32)).astype(BF16)

    carry = ssend[0].astype(F32)
    for i in range(1, GRP):
        ssend[i] = apply_map((pregam[i - 1], pre[i - 1]), carry).astype(BF16)
    for d in (2, 1, 3):
        c4(d).start()
    sgot[zlo] = ssend[zlo]

    @pl.when(last)
    def _():
        attend(3)

    kv_step(5)
    kc(4).wait_recv()
    attend(4)
    kv_step(6)
    kc(5).wait_recv()
    attend(5)
    kc(6).wait_recv()
    attend(6)
    moves[7].wait()
    for head in range(2):
        rows = slice(head * TOK, head * TOK + TOK)
        cols = slice(head * HA, head * HA + HA)
        gate = ag_ref[:, cols].astype(F32)
        read = acc[rows, :] / l_scr[rows, :]
        attn[:, cols] = (read / (1.0 + jnp.exp(-gate))).astype(BF16)

    moves[8].wait()
    for d in (1, 2, 3):
        c4(d).wait_recv()
    for h in range(4):
        cols = slice(h * DK, h * DK + DK)
        read = r0_s[h] + dot(qe_s[h], sgot[h])
        scale = lax.rsqrt(jnp.mean(read * read, 1, keepdims=True) + 1e-06)
        gate = og_ref[:, cols].astype(F32)
        silu = gate / (1.0 + jnp.exp(-gate))
        mixed[:, cols] = (read * scale * gain_ref[...] * silu).astype(BF16)

    for d in (1, 2, 3):
        wy_all(d).wait_recv()

    def copy(d):
        return remote(sbuf.at[d - 1], rbuf.at[d - 1], rss.at[d - 1], rsr.at[d - 1], mp_dev(d))

    def term(d):
        to = (mp + d) % 8
        half = pl.ds((to % 2) * 8, 8)
        first = wall[to // 2, half, 0].reshape(256, 512)
        second = wall[to // 2, half, 1].reshape(256, 512)
        return (dot_nt(mixed[...], first) + dot_nt(attn[...], second)).astype(BF16)

    order = (4, 3, 5, 2, 6, 1, 7)
    for d in order:
        sbuf[d - 1] = term(d)
        copy(d).start()
    total = term(0).astype(F32)
    for d in order:
        copy(d).wait_recv()
        total = total + rbuf[d - 1].astype(F32)
    out_ref[...] = total

    for d in (1, 2, 3):
        c1(d).wait_send()
        c4(d).wait_send()
        wy_all(d).wait_send()

        @pl.when(zhi + d < GRP)
        def _():
            c2(d).wait_send()

        @pl.when(last)
        def _():
            c3(d).wait_send()
            cc(d).wait_send()

    for s in range(1, SPAN + 1):
        kz(s).wait_send()
        kc(s).wait_send()
    for k in range(1, up_steps + 1):
        wz_up(k).wait_send()
        if k <= down_steps:
            wz_down(k).wait_send()
    for d in order:
        copy(d).wait_send()


def turn_table():
    table = np.zeros((8, 128), np.float32)
    freq = np.power(1e7, -2.0 * np.arange(ROT // 2) / ROT)
    table[0, : ROT // 2] = freq
    table[0, ROT // 2 : ROT] = freq
    table[1, : ROT // 2] = -1.0
    table[1, ROT // 2 : ROT] = 1.0
    return table


def per_device(
    residual,
    delta_query,
    delta_key,
    delta_value,
    write_strength,
    log_decay,
    output_gate,
    norm_gain,
    attn_query,
    attn_key,
    attn_value,
    attn_gate,
    positions,
    block_lists,
    out_weight,
):
    weight_rows = jnp.transpose(out_weight, (0, 2, 1))
    dma = pltpu.SemaphoreType.DMA
    summed = pl.pallas_call(
        mixer_kernel,
        out_shape=jax.ShapeDtypeStruct((TOK, 256), F32),
        in_specs=[ANY] * 9 + [VMEM] * 6,
        out_specs=VMEM,
        scratch_shapes=[
            pltpu.VMEM((YN, ZN, 2, 32, 512), BF16),
            pltpu.VMEM((TOK, 2 * DK), BF16),
            pltpu.VMEM((TOK, 2 * DK), BF16),
            pltpu.VMEM((TOK, 4 * DK), BF16),
            pltpu.VMEM((TOK, 2 * HA), BF16),
            pltpu.VMEM((TOK, 2 * HA), BF16),
            pltpu.VMEM((TOK, 2 * HA), BF16),
            pltpu.VMEM((TOK, 4 * DK), BF16),
            pltpu.VMEM((TOK, 2 * HA), BF16),
            pltpu.VMEM((4, TOK, TOK), F32),
            pltpu.VMEM((4, TOK, 2 * DK), BF16),
            pltpu.VMEM((4, TOK, TOK), BF16),
            pltpu.VMEM((4, TOK, DK), F32),
            pltpu.VMEM((4, TOK, DK), BF16),
            pltpu.VMEM((2 * TOK, HA), BF16),
            pltpu.VMEM((2, TOK, HA), BF16),
            pltpu.VMEM((GRP, MAPR, 2 * DK), BF16),
            pltpu.VMEM((GRP, MAPR, 2 * DK), BF16),
            pltpu.VMEM((GRP, MAPR, 2 * DK), BF16),
            pltpu.VMEM((YN, MAPR, 2 * DK), BF16),
            pltpu.VMEM((GRP - 1, DK, 2 * DK), F32),
            pltpu.VMEM((GRP - 1, 1, 2 * DK), F32),
            pltpu.VMEM((DK, 2 * DK), F32),
            pltpu.VMEM((1, 2 * DK), F32),
            pltpu.VMEM((DK, DK), BF16),
            pltpu.VMEM((DK, DK), BF16),
            pltpu.VMEM((GRP, DK, DK), BF16),
            pltpu.VMEM((GRP, DK, DK), BF16),
            pltpu.VMEM((SPAN, 2, TOK, HA), BF16),
            pltpu.VMEM((2 * TOK, 1), F32),
            pltpu.VMEM((2 * TOK, 1), F32),
            pltpu.VMEM((2 * TOK, HA), F32),
            pltpu.VMEM((TOK, 4 * DK), BF16),
            pltpu.VMEM((TOK, 2 * HA), BF16),
            pltpu.VMEM((7, TOK, 256), BF16),
            pltpu.VMEM((7, TOK, 256), BF16),
            dma((9,)),
        ]
        + [dma((3,))] * 6
        + [dma((3,)), dma]
        + [dma((3,))] * 2
        + [dma((SPAN,))] * 4
        + [dma((ZN // 2,))] * 4
        + [dma((3,))] * 2
        + [dma((7,))] * 2,
        compiler_params=pltpu.CompilerParams(
            vmem_limit_bytes=56 * MB, collective_id=1, has_side_effects=True
        ),
        name="mixer",
    )(
        weight_rows, delta_key, delta_query, delta_value, attn_key, attn_value, attn_query, output_gate, attn_gate,
        write_strength, log_decay, positions.reshape(1, TOK), block_lists, jnp.asarray(turn_table()), norm_gain.reshape(1, DK),
    )
    return (residual.astype(F32) + summed).astype(BF16)


def solution(mesh):
    return jax.shard_map(
        per_device,
        mesh=mesh,
        in_specs=(
            P("ctx", "mp"),
            P("ctx", "mp"),
            P("ctx", "mp"),
            P("ctx", "mp"),
            P("mp", "ctx"),
            P("mp", "ctx"),
            P("ctx", "mp"),
            P(),
            P("ctx", "mp"),
            P("ctx", None),
            P("ctx", None),
            P("ctx", "mp"),
            P("ctx"),
            P("ctx", None),
            P(None, "mp", "ctx"),
        ),
        out_specs=P("ctx", "mp"),
        check_vma=False,
    )
```

```python
import jax
import jax.numpy as jnp
import numpy as np
from jax import lax
from jax.experimental import pallas as pl
from jax.experimental.pallas import tpu as pltpu
from jax.sharding import PartitionSpec as P

DK = 128
AH = 16
KVH = 2
HA = 256
BLK = 128
SPAN = 6
ROT = 64
TOK = 256
ZN = 16
YN = 4
GRP = 4
MAPR = 144
WROWS = 64
QTR = 4
QROWS = TOK // QTR
GAPS = (
    ("k2", "a0", "w1"),
    ("w2", "w3", "k4"),
    ("w4", "a1"),
    ("w5", "w6", "k6", "w7", "a2"),
    ("w8", "a3", "a4", "a5", "a6"),
)
MESH = pl.DeviceIdType.MESH
F32 = jnp.float32
BF16 = jnp.bfloat16
ANY = pl.BlockSpec(memory_space=pl.ANY)
VMEM = pl.BlockSpec(memory_space=pltpu.VMEM)
MB = 1 << 20


def dot(a, b):
    return jnp.dot(a, b, preferred_element_type=F32)


def dot_nt(a, b):
    return lax.dot_general(a, b, (((1,), (1,)), ((), ())), preferred_element_type=F32)


def iota(shape, axis):
    return lax.broadcasted_iota(jnp.int32, shape, axis)


def base_inverse(lower):
    row = iota((TOK, 128), 0)
    lane = iota((TOK, 128), 1)
    left = jnp.where(row // 16 == lane // 16, lower[:, :128], 0.0)
    right = jnp.where(row // 16 == (lane + 128) // 16, lower[:, 128:], 0.0)
    folded = left + right
    for step in (64, 32, 16):
        folded = folded + pltpu.roll(folded, step, 1)
    low3 = folded.reshape(16, 16, 128)
    inv3 = jnp.where(row % 16 == lane % 16, 1.0, 0.0).astype(F32).reshape(16, 16, 128)
    for j in range(15):
        inv3 = inv3 - low3[:, :, j : j + 1] * inv3[:, j : j + 1, :]
    return inv3.reshape(TOK, 128)


def merge_blocks(lower, compact):
    r1 = iota((128, 128), 0)
    c1 = iota((128, 128), 1)
    halves = []
    for part in range(2):
        rows = slice(part * 128, part * 128 + 128)
        inv = jnp.where(r1 // 16 == c1 // 16, compact[rows], 0.0)
        low = lower[rows, rows]
        for size in (16, 32, 64):
            between = (r1 // (2 * size) == c1 // (2 * size)) & (r1 // size != c1 // size)
            off = jnp.where(between, low, 0.0)
            hi = inv.astype(BF16)
            inv = inv - dot(hi, dot(off.astype(BF16), hi).astype(BF16))
        halves.append(inv)
    inner = dot(lower[128:, :128].astype(BF16), halves[0].astype(BF16))
    cross = -dot(halves[1].astype(BF16), inner.astype(BF16))
    top = jnp.concatenate([halves[0], jnp.zeros((128, 128), F32)], 1)
    return jnp.concatenate([top, jnp.concatenate([cross, halves[1]], 1)], 0)


def gamma_rows(gamma):
    high = gamma.astype(BF16).astype(F32)
    middle = (gamma - high).astype(BF16).astype(F32)
    low = gamma - high - middle
    row = iota((16, gamma.shape[1]), 0)
    rows = jnp.where(row == 0, high, jnp.where(row == 1, middle, jnp.where(row == 2, low, 0.0)))
    return rows.astype(BF16)


def read_map(ref, index):
    tail = ref[index, DK:, :].astype(F32)
    gamma = tail[0:1] + tail[1:2] + tail[2:3]
    return gamma, ref[index, :DK, :].astype(F32)


def join(later, earlier):
    gl, xl = later
    ge, xe = earlier
    scaled = jnp.concatenate([xl[:, :DK] * ge[:, :DK], xl[:, DK:]], 1)
    return gl * ge, gl * xe + scaled - dot(xl[:, :DK].astype(BF16), xe.astype(BF16))


def apply_map(one, state):
    gamma, x = one
    return gamma[:, :DK] * state + x[:, DK:] - dot(x[:, :DK].astype(BF16), state.astype(BF16))


def write_map(ref, index, one):
    gamma, x = one
    ref[index, :DK, :] = x.astype(BF16)
    ref[index, DK:, :] = gamma_rows(gamma)


def mixer_kernel(
    w_hbm, dk_hbm, dq_hbm, dv_hbm, ak_hbm, av_hbm, aq_hbm, og_hbm, ag_hbm,
    wr_ref, ld_ref, pos_ref, list_ref, turn_ref, gain_ref,
    out_ref,
    wall, dk_ref, dq_ref, dv_ref, ak_ref, av_ref, aq_ref, og_ref, ag_ref,
    low_s, rhs_s, kts_s, both_s, reads_s, r0_s, qe_s, qrot, own,
    maps, l1, l2, l3, pre, pregam, prefix, prefgam, csend, cgot, ssend, sgot,
    kvbuf, m_scr, l_scr, acc, mixed, attn, tosib, fromsib, sbuf, rbuf,
    ins, s1, r1, s2, r2, s3, r3, sc, rc, s4, r4, kzs, kzr, kcs, kcr,
    wps, wpr, wms, wmr, wys, wyr, ps, pr, rss, rsr,
):
    c = lax.axis_index("ctx")
    mp = lax.axis_index("mp")
    y = c // ZN
    z = c % ZN
    zlo = z % GRP
    zhi = z // GRP
    core = mp % 2
    sibling = mp + 1 - 2 * core
    x = mp // 2
    quarter = mp % QTR

    def ctx_dev(d):
        return ((c + ZN * YN + d) % (ZN * YN), mp)

    z_up = (y * ZN + (z + 1) % ZN, mp)
    z_down = (y * ZN + (z + ZN - 1) % ZN, mp)

    def lo_peer(d):
        return (zlo + d) % GRP

    def lo_dev(d):
        return (y * ZN + zhi * GRP + lo_peer(d), mp)

    def hi_dev(d):
        return (y * ZN + ((zhi + d) % GRP) * GRP + zlo, mp)

    def y_dev(d):
        return (((y + d) % YN) * ZN + z, mp)

    def mp_dev(d):
        return (c, (mp + d) % 8)

    barrier = pltpu.get_barrier_semaphore()
    peers = [f(d) for f in (lo_dev, hi_dev, y_dev) for d in (1, 2, 3)] + [mp_dev(d) for d in range(1, 8)]
    peers += [ctx_dev(d) for d in (1, 2, -1, -2)] + [z_up, z_down]
    for peer in peers:
        pl.semaphore_signal(barrier, inc=1, device_id=peer, device_id_type=MESH)

    moves = [
        (w_hbm, wall.at[y, z]),
        (dk_hbm, dk_ref),
        (dq_hbm, dq_ref),
        (ak_hbm, ak_ref),
        (av_hbm, av_ref),
        (dv_hbm, dv_ref),
        (aq_hbm, aq_ref),
        (ag_hbm, ag_ref),
        (og_hbm, og_ref),
    ]
    moves = [pltpu.make_async_copy(src, dst, ins.at[i]) for i, (src, dst) in enumerate(moves)]
    for move in moves:
        move.start()

    def remote(src, dst, send, recv, device):
        return pltpu.make_async_remote_copy(
            src_ref=src, dst_ref=dst, send_sem=send, recv_sem=recv, device_id=device, device_id_type=MESH
        )

    def c1(d):
        return remote(maps.at[lo_peer(d)], l1.at[zlo], s1.at[d - 1], r1.at[d - 1], lo_dev(d))

    def c2(d):
        return remote(l2.at[zhi], l2.at[zhi], s2.at[d - 1], r2.at[d - 1], hi_dev(d))

    def c3(d):
        return remote(l3.at[y], l3.at[y], s3.at[d - 1], r3.at[d - 1], y_dev(d))

    def cc(d):
        return remote(csend, cgot, sc.at[d - 1], rc, hi_dev(d))

    def c4(d):
        return remote(ssend.at[lo_peer(d)], sgot.at[zlo], s4.at[d - 1], r4.at[d - 1], lo_dev(d))

    def kz(s):
        odd = s % 2
        src = own.at[quarter] if s <= 2 else kvbuf.at[s - 2 if odd else s - 3, quarter]
        return remote(src, kvbuf.at[s - 1, quarter], kzs.at[s - 1], kzr.at[s - 1], ctx_dev(1 if odd else 2))

    def kc(s, d):
        block = kvbuf.at[s - 1, quarter]
        mate = (c, (mp // QTR) * QTR + (quarter + d) % QTR)
        return remote(block, block, kcs.at[s - 1, d - 1], kcr.at[s - 1, d - 1], mate)

    def kv_stage(s):
        kz(s).wait_recv()
        if s < SPAN:
            kz(s + 2).start()
            kz(s + 1).start()
        for d in (2, 3, 1):
            kc(s, d).start()
        kz(s - 1).wait_recv()
        for d in (2, 3, 1):
            kc(s - 1, d).start()

    def kv_ready(s):
        for d in (1, 2, 3):
            kc(s, d).wait_recv()

    def ring(block, k, sems):
        up = block((z + ZN - k + 1) % ZN)
        down = block((z + k - 1) % ZN)
        return (
            lambda: remote(up, up, sems[0].at[k - 1], sems[1].at[k - 1], z_up),
            lambda: remote(down, down, sems[2].at[k - 1], sems[3].at[k - 1], z_down),
        )

    up_steps, down_steps = ZN // 2, ZN // 2 - 1

    def ring_b(k):
        return ring(lambda zs: wall.at[y, zs], k, (wps, wpr, wms, wmr))

    def wy_send(zs):
        for d in (2, 1, 3):
            block = wall.at[y, zs]
            remote(block, block, wys.at[d - 1], wyr.at[d - 1], y_dev(d)).start()

    def wy_all(d):
        return remote(wall.at[y], wall.at[y], wys.at[d - 1], wyr.at[d - 1], y_dev(d))

    def step_ring(which, k):
        up, down = which(k)
        further = which(k + 1) if k < up_steps else None
        up().wait_recv()
        if k < up_steps:
            further[0]().start()
        if k <= down_steps:
            down().wait_recv()
            if k < down_steps:
                further[1]().start()

    def w_start():
        for copy in ring_b(1):
            copy().start()
        wy_send(z)

    def w_step(k):
        step_ring(ring_b, k)
        wy_send((z + ZN - k) % ZN)
        if k <= down_steps:
            wy_send((z + k) % ZN)

    rr = iota((TOK, TOK), 0)
    cc2 = iota((TOK, TOK), 1)
    upto = rr >= cc2
    strict = rr > cc2
    diag = rr == cc2
    tri = jnp.where(rr <= cc2, 1.0, 0.0).astype(F32)
    exact = lax.Precision.HIGHEST
    g_rows = jnp.dot(ld_ref[...], tri, precision=exact, preferred_element_type=F32)
    g_cols = jnp.transpose(jnp.concatenate([g_rows, g_rows], 0))
    b_cols = jnp.transpose(jnp.concatenate([wr_ref[...], wr_ref[...]], 0))
    place = jnp.transpose(jnp.broadcast_to(pos_ref[...].astype(F32), (8, TOK)))[:, 0:1]
    angle = place * turn_ref[0:1, :]
    cosine = jnp.cos(angle)
    sine = jnp.sin(angle) * turn_ref[1:2, :]
    lane = iota((TOK, 128), 1)

    def rotate(x):
        swapped = jnp.where(lane < ROT // 2, pltpu.roll(x, 128 - ROT // 2, 1), pltpu.roll(x, ROT // 2, 1))
        return x * cosine + swapped * sine

    moves[1].wait()
    moves[2].wait()
    rq_cols = []
    for kh in range(2):
        cols = slice(kh * DK, kh * DK + DK)
        kb = dk_ref[:, cols]
        qb = dq_ref[:, cols]
        qf = qb.astype(F32)
        gram = dot_nt(kb, kb)
        cross = dot_nt(qb, kb)
        square = jnp.where(diag, gram, 0.0)
        rk_col = lax.rsqrt(jnp.sum(square, 1, keepdims=True) + 1e-06)
        rk_row = lax.rsqrt(jnp.sum(square, 0, keepdims=True) + 1e-06)
        rq_col = lax.rsqrt(jnp.sum(qf * qf, 1, keepdims=True) + 1e-06)
        rq_cols.append(rq_col)
        kf = kb.astype(F32)
        kt = jnp.transpose(kf)
        for h in (2 * kh, 2 * kh + 1):
            g_row = g_rows[h : h + 1]
            g_col = g_cols[:, h : h + 1]
            b_col = b_cols[:, h : h + 1]
            rhs_s[h, :, :DK] = (kf * (b_col * jnp.exp(g_col) * rk_col)).astype(BF16)
            kts_s[h] = (kt * (jnp.exp(g_row[:, TOK - 1 :] - g_row) * rk_row)).astype(BF16)
            spread = g_cols[:, h : h + 1] - g_rows[h : h + 1]
            fade = jnp.where(upto, jnp.exp(jnp.where(upto, spread, 0.0)), 0.0)
            low_s[h] = jnp.where(strict, fade * gram, 0.0) * (b_cols[:, h : h + 1] * rk_col) * rk_row
            reads_s[h] = (fade * cross * rq_col * rk_row).astype(BF16)

    moves[3].wait()
    moves[4].wait()
    pair = mp // 4
    keys = jnp.where(pair == 0, ak_ref[:, :HA], ak_ref[:, HA:])
    values = jnp.where(pair == 0, av_ref[:, :HA], av_ref[:, HA:])
    turned = rotate(keys[:, :128].astype(F32)).astype(BF16)
    for q in range(QTR):
        rows = slice(q * QROWS, q * QROWS + QROWS)
        own[q, :QROWS, :128] = turned[rows]
        own[q, :QROWS, 128:] = keys[rows, 128:]
        own[q, QROWS:, :] = values[rows]

    moves[0].wait()
    pl.semaphore_wait(barrier, len(peers))
    w_start()
    kz(2).start()
    kz(1).start()

    moves[5].wait()
    for h in range(4):
        values = dv_ref[:, h * DK : h * DK + DK].astype(F32)
        rhs_s[h, :, DK:] = (values * b_cols[:, h : h + 1]).astype(BF16)
    bases = [base_inverse(low_s[h]) for h in range(4)]
    inverses = [merge_blocks(low_s[h], bases[h]) for h in range(4)]
    for h in range(4):
        both = dot(inverses[h].astype(BF16), rhs_s[h]).astype(BF16)
        both_s[h] = both
        maps[h, :DK, :] = dot(kts_s[h], both).astype(BF16)
        maps[h, DK:, :] = gamma_rows(jnp.broadcast_to(jnp.exp(g_cols[TOK - 1 :, h : h + 1]), (1, 2 * DK)))
    for d in (2, 1, 3):
        c1(d).start()
    l1[zlo] = maps[zlo]
    for h in range(4):
        cols = slice((h // 2) * DK, (h // 2) * DK + DK)
        seen = dot(reads_s[h], both_s[h])
        r0_s[h] = seen[:, DK:]
        qf = dq_ref[:, cols].astype(F32)
        qe_s[h] = (jnp.exp(g_cols[:, h : h + 1]) * rq_cols[h // 2] * qf - seen[:, :DK]).astype(BF16)
    moves[6].wait()
    for head in range(2):
        rows = slice(head * TOK, head * TOK + TOK)
        first = aq_ref[:, head * HA : head * HA + 128].astype(F32)
        qrot[rows, :128] = rotate(first).astype(BF16) * BF16(1.0 / 16)
        qrot[rows, 128:] = aq_ref[:, head * HA + 128 : head * HA + HA] * BF16(1.0 / 16)
    entries = list_ref[...]
    row16 = iota((16, TOK), 0)
    candidate = (c - row16 // 2) * 2 + iota((16, TOK), 1) // BLK
    hit = jnp.zeros((16, TOK), F32)
    for e in range(entries.shape[1]):
        entry = jnp.where(row16 % 2 == 0, entries[0:1, e : e + 1], entries[1:2, e : e + 1])
        hit = jnp.where(candidate == entry, 1.0, hit)
    bias16 = jnp.where((hit > 0.5) & (candidate >= 0), 0.0, -1e30)

    def attend(s):
        first = s == 0
        packed = own[...] if first else kvbuf[s - 1]
        score = dot_nt(qrot[...], packed[:, :QROWS].reshape(TOK, HA))
        rows = bias16[2 * s : 2 * s + 2, :]
        bias = jnp.concatenate(
            [jnp.broadcast_to(rows[qb : qb + 1], (BLK, TOK)) for _ in range(2) for qb in range(2)], 0
        )
        score = score + bias
        if first:
            r = iota((2 * TOK, TOK), 0) % TOK
            score = jnp.where(iota((2 * TOK, TOK), 1) <= r, score, -1e30)
        top = jnp.max(score, 1, keepdims=True)
        if not first:
            old = m_scr[...]
            top = jnp.maximum(old, top)
            fade = jnp.exp(old - top)
        weights = jnp.exp(score - top)
        total = jnp.sum(weights, 1, keepdims=True)
        part = dot(weights.astype(BF16), packed[:, QROWS:].reshape(TOK, HA))
        m_scr[...] = top
        if first:
            l_scr[...] = total
            acc[...] = part
        else:
            l_scr[...] = l_scr[...] * fade + total
            acc[...] = acc[...] * fade + part

    def fill(gap):
        for item in GAPS[gap]:
            kind, number = item[0], int(item[1])
            if kind == "w":
                w_step(number)
            elif kind == "k":
                kv_stage(number)
            else:
                if number:
                    kv_ready(number)
                attend(number)

    fill(0)
    for d in (1, 2, 3):
        c1(d).wait_recv()
    parts = [read_map(l1, i) for i in range(GRP)]
    early = join(parts[1], parts[0])
    write_map(l2, zhi, join(join(parts[3], parts[2]), early))
    for d in (1, 2, 3):

        @pl.when(zhi + d < GRP)
        def _():
            c2(d).start()

    for i, one in enumerate((parts[0], early, join(parts[2], early))):
        pregam[i] = one[0]
        pre[i] = one[1]
    fill(1)

    for d in (1, 2, 3):

        @pl.when(zhi >= d)
        def _():
            c2(d).wait_recv()

    def put_prefix(one):
        prefgam[...] = one[0]
        prefix[...] = one[1]

    @pl.when(zhi == 1)
    def _():
        put_prefix(read_map(l2, 0))

    @pl.when(zhi == 2)
    def _():
        put_prefix(join(read_map(l2, 1), read_map(l2, 0)))

    last = zhi == GRP - 1

    @pl.when(last)
    def _():
        parts = [read_map(l2, i) for i in range(GRP)]
        early = join(parts[1], parts[0])
        write_map(l3, y, join(join(parts[3], parts[2]), early))
        for d in (2, 1, 3):
            c3(d).start()
        put_prefix(join(parts[2], early))

    fill(2)

    @pl.when(last)
    def _():
        for d in (1, 2, 3):
            c3(d).wait_recv()
        state = read_map(l3, 0)[1][:, DK:]
        carry = jnp.where(y == 1, state, 0.0)
        for i in range(1, YN - 1):
            state = apply_map(read_map(l3, i), state)
            carry = jnp.where(y == i + 1, state, carry)
        csend[...] = carry.astype(BF16)
        for d in (2, 1, 3):
            cc(d).start()

    @pl.when(zhi > 0)
    def _():
        ahead = (prefgam[...], prefix[...])
        for i in range(GRP - 1):
            one = join((pregam[i], pre[i]), ahead)
            pregam[i] = one[0]
            pre[i] = one[1]

    fill(3)

    @pl.when(jnp.logical_not(last))
    def _():
        remote(csend, cgot, sc.at[0], rc, hi_dev(1)).wait_recv()

    @pl.when(last)
    def _():
        cgot[...] = csend[...]

    ssend[0] = cgot[...]
    carry = cgot[...].astype(F32)

    @pl.when(zhi > 0)
    def _():
        ssend[0] = apply_map((prefgam[...], prefix[...]), carry).astype(BF16)

    for i in range(1, GRP):
        ssend[i] = apply_map((pregam[i - 1], pre[i - 1]), carry).astype(BF16)
    for d in (2, 1, 3):
        c4(d).start()
    sgot[zlo] = ssend[zlo]
    fill(4)
    moves[7].wait()
    for head in range(2):
        rows = slice(head * TOK, head * TOK + TOK)
        cols = slice(head * HA, head * HA + HA)
        gate = ag_ref[:, cols].astype(F32)
        read = acc[rows, :] / l_scr[rows, :]
        attn[:, cols] = (read / (1.0 + jnp.exp(-gate))).astype(BF16)

    moves[8].wait()
    for d in (1, 2, 3):
        c4(d).wait_recv()
    for h in range(4):
        cols = slice(h * DK, h * DK + DK)
        read = r0_s[h] + dot(qe_s[h], sgot[h])
        scale = lax.rsqrt(jnp.mean(read * read, 1, keepdims=True) + 1e-06)
        gate = og_ref[:, cols].astype(F32)
        silu = gate / (1.0 + jnp.exp(-gate))
        mixed[:, cols] = (read * scale * gain_ref[...] * silu).astype(BF16)

    for d in (1, 2, 3):
        wy_all(d).wait_recv()

    def x_copy(d):
        peer = (c, ((x + d) % 4) * 2 + core)
        return remote(sbuf.at[d - 1], rbuf.at[d - 1], rss.at[d - 1], rsr.at[d - 1], peer)

    def sib_copy(d):
        return remote(tosib.at[d], fromsib.at[d], ps.at[d], pr.at[d], (c, sibling))

    def term(d, side):
        to = ((x + d) % 4) * 2 + side
        half = pl.ds(side * 8, 8)
        first = wall[to // 2, half, :32].reshape(256, 512)
        second = wall[to // 2, half, 32:].reshape(256, 512)
        return dot_nt(mixed[...], first) + dot_nt(attn[...], second)

    order = (2, 1, 3, 0)
    for d in order:
        tosib[d] = term(d, 1 - core).astype(BF16)
        sib_copy(d).start()
    for d in order[:3]:
        mine = term(d, core)
        sib_copy(d).wait_recv()
        sbuf[d - 1] = (mine + fromsib[d].astype(F32)).astype(BF16)
        x_copy(d).start()
    total = term(0, core)
    sib_copy(0).wait_recv()
    total = total + fromsib[0].astype(F32)
    for d in order[:3]:
        x_copy(d).wait_recv()
        total = total + rbuf[d - 1].astype(F32)
    out_ref[...] = total

    for d in (1, 2, 3):
        c1(d).wait_send()
        c4(d).wait_send()
        wy_all(d).wait_send()

        @pl.when(zhi + d < GRP)
        def _():
            c2(d).wait_send()

        @pl.when(last)
        def _():
            c3(d).wait_send()
            cc(d).wait_send()

    for s in range(1, SPAN + 1):
        kz(s).wait_send()
        for d in (1, 2, 3):
            kc(s, d).wait_send()
    for d in (1, 2, 3):
        x_copy(d).wait_send()
    for k in range(1, up_steps + 1):
        up, down = ring_b(k)
        up().wait_send()
        if k <= down_steps:
            down().wait_send()
    for d in order:
        sib_copy(d).wait_send()


def turn_table():
    table = np.zeros((8, 128), np.float32)
    freq = np.power(1e7, -2.0 * np.arange(ROT // 2) / ROT)
    table[0, : ROT // 2] = freq
    table[0, ROT // 2 : ROT] = freq
    table[1, : ROT // 2] = -1.0
    table[1, ROT // 2 : ROT] = 1.0
    return table


def per_device(
    residual,
    delta_query,
    delta_key,
    delta_value,
    write_strength,
    log_decay,
    output_gate,
    norm_gain,
    attn_query,
    attn_key,
    attn_value,
    attn_gate,
    positions,
    block_lists,
    out_weight,
):
    weight_rows = jnp.transpose(out_weight, (0, 2, 1)).reshape(WROWS, 512)
    dma = pltpu.SemaphoreType.DMA
    summed = pl.pallas_call(
        mixer_kernel,
        out_shape=jax.ShapeDtypeStruct((TOK, 256), F32),
        in_specs=[ANY] * 9 + [VMEM] * 6,
        out_specs=VMEM,
        scratch_shapes=[
            pltpu.VMEM((YN, ZN, WROWS, 512), BF16),
            pltpu.VMEM((TOK, 2 * DK), BF16),
            pltpu.VMEM((TOK, 2 * DK), BF16),
            pltpu.VMEM((TOK, 4 * DK), BF16),
            pltpu.VMEM((TOK, 2 * HA), BF16),
            pltpu.VMEM((TOK, 2 * HA), BF16),
            pltpu.VMEM((TOK, 2 * HA), BF16),
            pltpu.VMEM((TOK, 4 * DK), BF16),
            pltpu.VMEM((TOK, 2 * HA), BF16),
            pltpu.VMEM((4, TOK, TOK), F32),
            pltpu.VMEM((4, TOK, 2 * DK), BF16),
            pltpu.VMEM((4, DK, TOK), BF16),
            pltpu.VMEM((4, TOK, 2 * DK), BF16),
            pltpu.VMEM((4, TOK, TOK), BF16),
            pltpu.VMEM((4, TOK, DK), F32),
            pltpu.VMEM((4, TOK, DK), BF16),
            pltpu.VMEM((2 * TOK, HA), BF16),
            pltpu.VMEM((QTR, 2 * QROWS, HA), BF16),
            pltpu.VMEM((GRP, MAPR, 2 * DK), BF16),
            pltpu.VMEM((GRP, MAPR, 2 * DK), BF16),
            pltpu.VMEM((GRP, MAPR, 2 * DK), BF16),
            pltpu.VMEM((YN, MAPR, 2 * DK), BF16),
            pltpu.VMEM((GRP - 1, DK, 2 * DK), F32),
            pltpu.VMEM((GRP - 1, 1, 2 * DK), F32),
            pltpu.VMEM((DK, 2 * DK), F32),
            pltpu.VMEM((1, 2 * DK), F32),
            pltpu.VMEM((DK, DK), BF16),
            pltpu.VMEM((DK, DK), BF16),
            pltpu.VMEM((GRP, DK, DK), BF16),
            pltpu.VMEM((GRP, DK, DK), BF16),
            pltpu.VMEM((SPAN, QTR, 2 * QROWS, HA), BF16),
            pltpu.VMEM((2 * TOK, 1), F32),
            pltpu.VMEM((2 * TOK, 1), F32),
            pltpu.VMEM((2 * TOK, HA), F32),
            pltpu.VMEM((TOK, 4 * DK), BF16),
            pltpu.VMEM((TOK, 2 * HA), BF16),
            pltpu.VMEM((4, TOK, 256), BF16),
            pltpu.VMEM((4, TOK, 256), BF16),
            pltpu.VMEM((3, TOK, 256), BF16),
            pltpu.VMEM((3, TOK, 256), BF16),
            dma((9,)),
        ]
        + [dma((3,))] * 6
        + [dma((3,)), dma]
        + [dma((3,))] * 2
        + [dma((SPAN,))] * 2
        + [dma((SPAN, 3))] * 2
        + [dma((ZN // 2,))] * 4
        + [dma((3,))] * 2
        + [dma((4,))] * 2
        + [dma((3,))] * 2,
        compiler_params=pltpu.CompilerParams(
            vmem_limit_bytes=56 * MB, collective_id=1, has_side_effects=True
        ),
        name="mixer",
    )(
        weight_rows, delta_key, delta_query, delta_value, attn_key, attn_value, attn_query, output_gate, attn_gate,
        write_strength, log_decay, positions.reshape(1, TOK), block_lists, jnp.asarray(turn_table()), norm_gain.reshape(1, DK),
    )
    return (residual.astype(F32) + summed).astype(BF16)


def solution(mesh):
    return jax.shard_map(
        per_device,
        mesh=mesh,
        in_specs=(
            P("ctx", "mp"),
            P("ctx", "mp"),
            P("ctx", "mp"),
            P("ctx", "mp"),
            P("mp", "ctx"),
            P("mp", "ctx"),
            P("ctx", "mp"),
            P(),
            P("ctx", "mp"),
            P("ctx", None),
            P("ctx", None),
            P("ctx", "mp"),
            P("ctx"),
            P("ctx", None),
            P(None, "mp", "ctx"),
        ),
        out_specs=P("ctx", "mp"),
        check_vma=False,
    )
```

```python
import jax
import jax.numpy as jnp
import numpy as np
from jax import lax
from jax.experimental import pallas as pl
from jax.experimental.pallas import tpu as pltpu
from jax.sharding import PartitionSpec as P

DK = 128
AH = 16
KVH = 2
HA = 256
BLK = 128
SPAN = 6
ROT = 64
TOK = 256
ZN = 16
YN = 4
GRP = 4
MAPR = 144
WROWS = 64
QTR = 4
QROWS = TOK // QTR
GAPS = (
    ("k2", "a0", "w1"),
    ("w2", "w3", "k4"),
    ("w4", "a1"),
    ("w5", "w6", "k6", "w7", "a2"),
    ("w8", "a3", "a4", "a5", "a6"),
)
MESH = pl.DeviceIdType.MESH
F32 = jnp.float32
BF16 = jnp.bfloat16
ANY = pl.BlockSpec(memory_space=pl.ANY)
VMEM = pl.BlockSpec(memory_space=pltpu.VMEM)
MB = 1 << 20


def dot(a, b):
    return jnp.dot(a, b, preferred_element_type=F32)


def dot_nt(a, b):
    return lax.dot_general(a, b, (((1,), (1,)), ((), ())), preferred_element_type=F32)


def iota(shape, axis):
    return lax.broadcasted_iota(jnp.int32, shape, axis)


def base_inverse(lower):
    row = iota((TOK, 128), 0)
    lane = iota((TOK, 128), 1)
    left = jnp.where(row // 16 == lane // 16, lower[:, :128], 0.0)
    right = jnp.where(row // 16 == (lane + 128) // 16, lower[:, 128:], 0.0)
    folded = left + right
    for step in (64, 32, 16):
        folded = folded + pltpu.roll(folded, step, 1)
    low3 = folded.reshape(16, 16, 128)
    inv3 = jnp.where(row % 16 == lane % 16, 1.0, 0.0).astype(F32).reshape(16, 16, 128)
    for j in range(15):
        inv3 = inv3 - low3[:, :, j : j + 1] * inv3[:, j : j + 1, :]
    return inv3.reshape(TOK, 128)


def merge_blocks(lower, compact):
    r1 = iota((128, 128), 0)
    c1 = iota((128, 128), 1)
    halves = []
    for part in range(2):
        rows = slice(part * 128, part * 128 + 128)
        inv = jnp.where(r1 // 16 == c1 // 16, compact[rows], 0.0)
        low = lower[rows, rows]
        for size in (16, 32, 64):
            between = (r1 // (2 * size) == c1 // (2 * size)) & (r1 // size != c1 // size)
            off = jnp.where(between, low, 0.0)
            hi = inv.astype(BF16)
            inv = inv - dot(hi, dot(off.astype(BF16), hi).astype(BF16))
        halves.append(inv)
    inner = dot(lower[128:, :128].astype(BF16), halves[0].astype(BF16))
    cross = -dot(halves[1].astype(BF16), inner.astype(BF16))
    top = jnp.concatenate([halves[0], jnp.zeros((128, 128), F32)], 1)
    return jnp.concatenate([top, jnp.concatenate([cross, halves[1]], 1)], 0)


def gamma_rows(gamma):
    high = gamma.astype(BF16).astype(F32)
    middle = (gamma - high).astype(BF16).astype(F32)
    low = gamma - high - middle
    row = iota((16, gamma.shape[1]), 0)
    rows = jnp.where(row == 0, high, jnp.where(row == 1, middle, jnp.where(row == 2, low, 0.0)))
    return rows.astype(BF16)


def read_map(ref, index):
    tail = ref[index, DK:, :].astype(F32)
    gamma = tail[0:1] + tail[1:2] + tail[2:3]
    return gamma, ref[index, :DK, :].astype(F32)


def join(later, earlier):
    gl, xl = later
    ge, xe = earlier
    scaled = jnp.concatenate([xl[:, :DK] * ge[:, :DK], xl[:, DK:]], 1)
    return gl * ge, gl * xe + scaled - dot(xl[:, :DK].astype(BF16), xe.astype(BF16))


def apply_map(one, state):
    gamma, x = one
    return gamma[:, :DK] * state + x[:, DK:] - dot(x[:, :DK].astype(BF16), state.astype(BF16))


def write_map(ref, index, one):
    gamma, x = one
    ref[index, :DK, :] = x.astype(BF16)
    ref[index, DK:, :] = gamma_rows(gamma)


def mixer_kernel(
    w_hbm, dk_hbm, dq_hbm, dv_hbm, ak_hbm, av_hbm, aq_hbm, og_hbm, ag_hbm,
    wr_ref, ld_ref, pos_ref, list_ref, turn_ref, gain_ref,
    out_ref,
    wall, dk_ref, dq_ref, dv_ref, ak_ref, av_ref, aq_ref, og_ref, ag_ref,
    low_s, rhs_s, kts_s, both_s, reads_s, r0_s, qe_s, qrot, own,
    maps, l1, l2, l3, pre, pregam, prefix, prefgam, csend, cgot, ssend, sgot,
    kvbuf, m_scr, l_scr, acc, mixed, attn, tosib, fromsib, sbuf, rbuf,
    ins, s1, r1, s2, r2, s3, r3, sc, rc, s4, r4, kzs, kzr, kcs, kcr,
    wps, wpr, wms, wmr, wys, wyr, ps, pr, rss, rsr,
):
    c = lax.axis_index("ctx")
    mp = lax.axis_index("mp")
    y = c // ZN
    z = c % ZN
    zlo = z % GRP
    zhi = z // GRP
    core = mp % 2
    sibling = mp + 1 - 2 * core
    x = mp // 2
    quarter = mp % QTR

    def ctx_dev(d):
        return ((c + ZN * YN + d) % (ZN * YN), mp)

    z_up = (y * ZN + (z + 1) % ZN, mp)
    z_down = (y * ZN + (z + ZN - 1) % ZN, mp)

    def lo_peer(d):
        return (zlo + d) % GRP

    def lo_dev(d):
        return (y * ZN + zhi * GRP + lo_peer(d), mp)

    def hi_dev(d):
        return (y * ZN + ((zhi + d) % GRP) * GRP + zlo, mp)

    def y_dev(d):
        return (((y + d) % YN) * ZN + z, mp)

    def mp_dev(d):
        return (c, (mp + d) % 8)

    barrier = pltpu.get_barrier_semaphore()
    peers = [f(d) for f in (lo_dev, hi_dev, y_dev) for d in (1, 2, 3)] + [mp_dev(d) for d in range(1, 8)]
    peers += [ctx_dev(d) for d in (1, 2, -1, -2)] + [z_up, z_down]
    for peer in peers:
        pl.semaphore_signal(barrier, inc=1, device_id=peer, device_id_type=MESH)

    moves = [
        (w_hbm, wall.at[y, z]),
        (dk_hbm, dk_ref),
        (dq_hbm, dq_ref),
        (ak_hbm, ak_ref),
        (av_hbm, av_ref),
        (dv_hbm, dv_ref),
        (aq_hbm, aq_ref),
        (ag_hbm, ag_ref),
        (og_hbm, og_ref),
    ]
    moves = [pltpu.make_async_copy(src, dst, ins.at[i]) for i, (src, dst) in enumerate(moves)]
    for move in moves:
        move.start()

    def remote(src, dst, send, recv, device):
        return pltpu.make_async_remote_copy(
            src_ref=src, dst_ref=dst, send_sem=send, recv_sem=recv, device_id=device, device_id_type=MESH
        )

    def c1(d):
        return remote(maps.at[lo_peer(d)], l1.at[zlo], s1.at[d - 1], r1.at[d - 1], lo_dev(d))

    def c2(d):
        return remote(l2.at[zhi], l2.at[zhi], s2.at[d - 1], r2.at[d - 1], hi_dev(d))

    def c3(d):
        return remote(l3.at[y], l3.at[y], s3.at[d - 1], r3.at[d - 1], y_dev(d))

    def cc(d):
        return remote(csend, cgot, sc.at[d - 1], rc, hi_dev(d))

    def c4(d):
        return remote(ssend.at[lo_peer(d)], sgot.at[zlo], s4.at[d - 1], r4.at[d - 1], lo_dev(d))

    def kz(s):
        odd = s % 2
        src = own.at[quarter] if s <= 2 else kvbuf.at[s - 2 if odd else s - 3, quarter]
        return remote(src, kvbuf.at[s - 1, quarter], kzs.at[s - 1], kzr.at[s - 1], ctx_dev(1 if odd else 2))

    def kc(s, d):
        block = kvbuf.at[s - 1, quarter]
        mate = (c, (mp // QTR) * QTR + (quarter + d) % QTR)
        return remote(block, block, kcs.at[s - 1, d - 1], kcr.at[s - 1, d - 1], mate)

    def kv_stage(s):
        kz(s).wait_recv()
        if s < SPAN:
            kz(s + 2).start()
            kz(s + 1).start()
        for d in (2, 3, 1):
            kc(s, d).start()
        kz(s - 1).wait_recv()
        for d in (2, 3, 1):
            kc(s - 1, d).start()

    def kv_ready(s):
        for d in (1, 2, 3):
            kc(s, d).wait_recv()

    def ring(block, k, sems):
        up = block((z + ZN - k + 1) % ZN)
        down = block((z + k - 1) % ZN)
        return (
            lambda: remote(up, up, sems[0].at[k - 1], sems[1].at[k - 1], z_up),
            lambda: remote(down, down, sems[2].at[k - 1], sems[3].at[k - 1], z_down),
        )

    up_steps, down_steps = ZN // 2, ZN // 2 - 1

    def ring_b(k):
        return ring(lambda zs: wall.at[y, zs], k, (wps, wpr, wms, wmr))

    def wy_send(zs):
        for d in (2, 1, 3):
            block = wall.at[y, zs]
            remote(block, block, wys.at[d - 1], wyr.at[d - 1], y_dev(d)).start()

    def wy_all(d):
        return remote(wall.at[y], wall.at[y], wys.at[d - 1], wyr.at[d - 1], y_dev(d))

    def step_ring(which, k):
        up, down = which(k)
        further = which(k + 1) if k < up_steps else None
        up().wait_recv()
        if k < up_steps:
            further[0]().start()
        if k <= down_steps:
            down().wait_recv()
            if k < down_steps:
                further[1]().start()

    def w_start():
        for copy in ring_b(1):
            copy().start()
        wy_send(z)

    def w_step(k):
        step_ring(ring_b, k)
        wy_send((z + ZN - k) % ZN)
        if k <= down_steps:
            wy_send((z + k) % ZN)

    moves[0].wait()
    pl.semaphore_wait(barrier, len(peers))
    w_start()

    rr = iota((TOK, TOK), 0)
    cc2 = iota((TOK, TOK), 1)
    upto = rr >= cc2
    strict = rr > cc2
    diag = rr == cc2
    tri = jnp.where(rr <= cc2, 1.0, 0.0).astype(F32)
    exact = lax.Precision.HIGHEST
    g_rows = jnp.dot(ld_ref[...], tri, precision=exact, preferred_element_type=F32)
    g_cols = jnp.transpose(jnp.concatenate([g_rows, g_rows], 0))
    b_cols = jnp.transpose(jnp.concatenate([wr_ref[...], wr_ref[...]], 0))
    place = jnp.transpose(jnp.broadcast_to(pos_ref[...].astype(F32), (8, TOK)))[:, 0:1]
    angle = place * turn_ref[0:1, :]
    cosine = jnp.cos(angle)
    sine = jnp.sin(angle) * turn_ref[1:2, :]
    lane = iota((TOK, 128), 1)

    def rotate(x):
        swapped = jnp.where(lane < ROT // 2, pltpu.roll(x, 128 - ROT // 2, 1), pltpu.roll(x, ROT // 2, 1))
        return x * cosine + swapped * sine

    moves[1].wait()
    moves[2].wait()
    rq_cols = []
    for kh in range(2):
        cols = slice(kh * DK, kh * DK + DK)
        kb = dk_ref[:, cols]
        qb = dq_ref[:, cols]
        qf = qb.astype(F32)
        gram = dot_nt(kb, kb)
        cross = dot_nt(qb, kb)
        square = jnp.where(diag, gram, 0.0)
        rk_col = lax.rsqrt(jnp.sum(square, 1, keepdims=True) + 1e-06)
        rk_row = lax.rsqrt(jnp.sum(square, 0, keepdims=True) + 1e-06)
        rq_col = lax.rsqrt(jnp.sum(qf * qf, 1, keepdims=True) + 1e-06)
        rq_cols.append(rq_col)
        kf = kb.astype(F32)
        kt = jnp.transpose(kf)
        for h in (2 * kh, 2 * kh + 1):
            g_row = g_rows[h : h + 1]
            g_col = g_cols[:, h : h + 1]
            b_col = b_cols[:, h : h + 1]
            rhs_s[h, :, :DK] = (kf * (b_col * jnp.exp(g_col) * rk_col)).astype(BF16)
            kts_s[h] = (kt * (jnp.exp(g_row[:, TOK - 1 :] - g_row) * rk_row)).astype(BF16)
            spread = g_cols[:, h : h + 1] - g_rows[h : h + 1]
            fade = jnp.where(upto, jnp.exp(jnp.where(upto, spread, 0.0)), 0.0)
            low_s[h] = jnp.where(strict, fade * gram, 0.0) * (b_cols[:, h : h + 1] * rk_col) * rk_row
            reads_s[h] = (fade * cross * rq_col * rk_row).astype(BF16)

    moves[3].wait()
    moves[4].wait()
    pair = mp // 4
    keys = jnp.where(pair == 0, ak_ref[:, :HA], ak_ref[:, HA:])
    values = jnp.where(pair == 0, av_ref[:, :HA], av_ref[:, HA:])
    turned = rotate(keys[:, :128].astype(F32)).astype(BF16)
    for q in range(QTR):
        rows = slice(q * QROWS, q * QROWS + QROWS)
        own[q, :QROWS, :128] = turned[rows]
        own[q, :QROWS, 128:] = keys[rows, 128:]
        own[q, QROWS:, :] = values[rows]

    kz(2).start()
    kz(1).start()

    moves[5].wait()
    for h in range(4):
        values = dv_ref[:, h * DK : h * DK + DK].astype(F32)
        rhs_s[h, :, DK:] = (values * b_cols[:, h : h + 1]).astype(BF16)
    bases = [base_inverse(low_s[h]) for h in range(4)]
    inverses = [merge_blocks(low_s[h], bases[h]) for h in range(4)]
    for h in range(4):
        both = dot(inverses[h].astype(BF16), rhs_s[h]).astype(BF16)
        both_s[h] = both
        maps[h, :DK, :] = dot(kts_s[h], both).astype(BF16)
        maps[h, DK:, :] = gamma_rows(jnp.broadcast_to(jnp.exp(g_cols[TOK - 1 :, h : h + 1]), (1, 2 * DK)))
    for d in (2, 1, 3):
        c1(d).start()
    l1[zlo] = maps[zlo]
    for h in range(4):
        cols = slice((h // 2) * DK, (h // 2) * DK + DK)
        seen = dot(reads_s[h], both_s[h])
        r0_s[h] = seen[:, DK:]
        qf = dq_ref[:, cols].astype(F32)
        qe_s[h] = (jnp.exp(g_cols[:, h : h + 1]) * rq_cols[h // 2] * qf - seen[:, :DK]).astype(BF16)
    moves[6].wait()
    for head in range(2):
        rows = slice(head * TOK, head * TOK + TOK)
        first = aq_ref[:, head * HA : head * HA + 128].astype(F32)
        qrot[rows, :128] = rotate(first).astype(BF16) * BF16(1.0 / 16)
        qrot[rows, 128:] = aq_ref[:, head * HA + 128 : head * HA + HA] * BF16(1.0 / 16)
    entries = list_ref[...]
    row16 = iota((16, TOK), 0)
    candidate = (c - row16 // 2) * 2 + iota((16, TOK), 1) // BLK
    hit = jnp.zeros((16, TOK), F32)
    for e in range(entries.shape[1]):
        entry = jnp.where(row16 % 2 == 0, entries[0:1, e : e + 1], entries[1:2, e : e + 1])
        hit = jnp.where(candidate == entry, 1.0, hit)
    bias16 = jnp.where((hit > 0.5) & (candidate >= 0), 0.0, -1e30)

    def attend(s):
        first = s == 0
        packed = own[...] if first else kvbuf[s - 1]
        score = dot_nt(qrot[...], packed[:, :QROWS].reshape(TOK, HA))
        rows = bias16[2 * s : 2 * s + 2, :]
        bias = jnp.concatenate(
            [jnp.broadcast_to(rows[qb : qb + 1], (BLK, TOK)) for _ in range(2) for qb in range(2)], 0
        )
        score = score + bias
        if first:
            r = iota((2 * TOK, TOK), 0) % TOK
            score = jnp.where(iota((2 * TOK, TOK), 1) <= r, score, -1e30)
        top = jnp.max(score, 1, keepdims=True)
        if not first:
            old = m_scr[...]
            top = jnp.maximum(old, top)
            fade = jnp.exp(old - top)
        weights = jnp.exp(score - top)
        total = jnp.sum(weights, 1, keepdims=True)
        part = dot(weights.astype(BF16), packed[:, QROWS:].reshape(TOK, HA))
        m_scr[...] = top
        if first:
            l_scr[...] = total
            acc[...] = part
        else:
            l_scr[...] = l_scr[...] * fade + total
            acc[...] = acc[...] * fade + part

    def fill(gap):
        for item in GAPS[gap]:
            kind, number = item[0], int(item[1])
            if kind == "w":
                w_step(number)
            elif kind == "k":
                kv_stage(number)
            else:
                if number:
                    kv_ready(number)
                attend(number)

    fill(0)
    for d in (1, 2, 3):
        c1(d).wait_recv()
    parts = [read_map(l1, i) for i in range(GRP)]
    early = join(parts[1], parts[0])
    write_map(l2, zhi, join(join(parts[3], parts[2]), early))
    for d in (1, 2, 3):

        @pl.when(zhi + d < GRP)
        def _():
            c2(d).start()

    for i, one in enumerate((parts[0], early, join(parts[2], early))):
        pregam[i] = one[0]
        pre[i] = one[1]
    fill(1)

    for d in (1, 2, 3):

        @pl.when(zhi >= d)
        def _():
            c2(d).wait_recv()

    def put_prefix(one):
        prefgam[...] = one[0]
        prefix[...] = one[1]

    @pl.when(zhi == 1)
    def _():
        put_prefix(read_map(l2, 0))

    @pl.when(zhi == 2)
    def _():
        put_prefix(join(read_map(l2, 1), read_map(l2, 0)))

    last = zhi == GRP - 1

    @pl.when(last)
    def _():
        parts = [read_map(l2, i) for i in range(GRP)]
        early = join(parts[1], parts[0])
        write_map(l3, y, join(join(parts[3], parts[2]), early))
        for d in (2, 1, 3):
            c3(d).start()
        put_prefix(join(parts[2], early))

    fill(2)

    @pl.when(last)
    def _():
        for d in (1, 2, 3):
            c3(d).wait_recv()
        state = read_map(l3, 0)[1][:, DK:]
        carry = jnp.where(y == 1, state, 0.0)
        for i in range(1, YN - 1):
            state = apply_map(read_map(l3, i), state)
            carry = jnp.where(y == i + 1, state, carry)
        csend[...] = carry.astype(BF16)
        for d in (2, 1, 3):
            cc(d).start()

    @pl.when(zhi > 0)
    def _():
        ahead = (prefgam[...], prefix[...])
        for i in range(GRP - 1):
            one = join((pregam[i], pre[i]), ahead)
            pregam[i] = one[0]
            pre[i] = one[1]

    fill(3)

    @pl.when(jnp.logical_not(last))
    def _():
        remote(csend, cgot, sc.at[0], rc, hi_dev(1)).wait_recv()

    @pl.when(last)
    def _():
        cgot[...] = csend[...]

    ssend[0] = cgot[...]
    carry = cgot[...].astype(F32)

    @pl.when(zhi > 0)
    def _():
        ssend[0] = apply_map((prefgam[...], prefix[...]), carry).astype(BF16)

    for i in range(1, GRP):
        ssend[i] = apply_map((pregam[i - 1], pre[i - 1]), carry).astype(BF16)
    for d in (2, 1, 3):
        c4(d).start()
    sgot[zlo] = ssend[zlo]
    fill(4)
    moves[7].wait()
    for head in range(2):
        rows = slice(head * TOK, head * TOK + TOK)
        cols = slice(head * HA, head * HA + HA)
        gate = ag_ref[:, cols].astype(F32)
        read = acc[rows, :] / l_scr[rows, :]
        attn[:, cols] = (read / (1.0 + jnp.exp(-gate))).astype(BF16)

    moves[8].wait()
    for d in (1, 2, 3):
        c4(d).wait_recv()
    for h in range(4):
        cols = slice(h * DK, h * DK + DK)
        read = r0_s[h] + dot(qe_s[h], sgot[h])
        scale = lax.rsqrt(jnp.mean(read * read, 1, keepdims=True) + 1e-06)
        gate = og_ref[:, cols].astype(F32)
        silu = gate / (1.0 + jnp.exp(-gate))
        mixed[:, cols] = (read * scale * gain_ref[...] * silu).astype(BF16)

    for d in (1, 2, 3):
        wy_all(d).wait_recv()

    def x_copy(d):
        peer = (c, ((x + d) % 4) * 2 + core)
        return remote(sbuf.at[d - 1], rbuf.at[d - 1], rss.at[d - 1], rsr.at[d - 1], peer)

    def sib_copy(d):
        return remote(tosib.at[d], fromsib.at[d], ps.at[d], pr.at[d], (c, sibling))

    def term(d, side):
        to = ((x + d) % 4) * 2 + side
        half = pl.ds(side * 8, 8)
        first = wall[to // 2, half, :32].reshape(256, 512)
        second = wall[to // 2, half, 32:].reshape(256, 512)
        return dot_nt(mixed[...], first) + dot_nt(attn[...], second)

    order = (2, 1, 3, 0)
    for d in order:
        tosib[d] = term(d, 1 - core).astype(BF16)
        sib_copy(d).start()
    for d in order[:3]:
        mine = term(d, core)
        sib_copy(d).wait_recv()
        sbuf[d - 1] = (mine + fromsib[d].astype(F32)).astype(BF16)
        x_copy(d).start()
    total = term(0, core)
    sib_copy(0).wait_recv()
    total = total + fromsib[0].astype(F32)
    for d in order[:3]:
        x_copy(d).wait_recv()
        total = total + rbuf[d - 1].astype(F32)
    out_ref[...] = total

    for d in (1, 2, 3):
        c1(d).wait_send()
        c4(d).wait_send()
        wy_all(d).wait_send()

        @pl.when(zhi + d < GRP)
        def _():
            c2(d).wait_send()

        @pl.when(last)
        def _():
            c3(d).wait_send()
            cc(d).wait_send()

    for s in range(1, SPAN + 1):
        kz(s).wait_send()
        for d in (1, 2, 3):
            kc(s, d).wait_send()
    for d in (1, 2, 3):
        x_copy(d).wait_send()
    for k in range(1, up_steps + 1):
        up, down = ring_b(k)
        up().wait_send()
        if k <= down_steps:
            down().wait_send()
    for d in order:
        sib_copy(d).wait_send()


def turn_table():
    table = np.zeros((8, 128), np.float32)
    freq = np.power(1e7, -2.0 * np.arange(ROT // 2) / ROT)
    table[0, : ROT // 2] = freq
    table[0, ROT // 2 : ROT] = freq
    table[1, : ROT // 2] = -1.0
    table[1, ROT // 2 : ROT] = 1.0
    return table


def per_device(
    residual,
    delta_query,
    delta_key,
    delta_value,
    write_strength,
    log_decay,
    output_gate,
    norm_gain,
    attn_query,
    attn_key,
    attn_value,
    attn_gate,
    positions,
    block_lists,
    out_weight,
):
    weight_rows = jnp.transpose(out_weight, (0, 2, 1)).reshape(WROWS, 512)
    dma = pltpu.SemaphoreType.DMA
    summed = pl.pallas_call(
        mixer_kernel,
        out_shape=jax.ShapeDtypeStruct((TOK, 256), F32),
        in_specs=[ANY] * 9 + [VMEM] * 6,
        out_specs=VMEM,
        scratch_shapes=[
            pltpu.VMEM((YN, ZN, WROWS, 512), BF16),
            pltpu.VMEM((TOK, 2 * DK), BF16),
            pltpu.VMEM((TOK, 2 * DK), BF16),
            pltpu.VMEM((TOK, 4 * DK), BF16),
            pltpu.VMEM((TOK, 2 * HA), BF16),
            pltpu.VMEM((TOK, 2 * HA), BF16),
            pltpu.VMEM((TOK, 2 * HA), BF16),
            pltpu.VMEM((TOK, 4 * DK), BF16),
            pltpu.VMEM((TOK, 2 * HA), BF16),
            pltpu.VMEM((4, TOK, TOK), F32),
            pltpu.VMEM((4, TOK, 2 * DK), BF16),
            pltpu.VMEM((4, DK, TOK), BF16),
            pltpu.VMEM((4, TOK, 2 * DK), BF16),
            pltpu.VMEM((4, TOK, TOK), BF16),
            pltpu.VMEM((4, TOK, DK), F32),
            pltpu.VMEM((4, TOK, DK), BF16),
            pltpu.VMEM((2 * TOK, HA), BF16),
            pltpu.VMEM((QTR, 2 * QROWS, HA), BF16),
            pltpu.VMEM((GRP, MAPR, 2 * DK), BF16),
            pltpu.VMEM((GRP, MAPR, 2 * DK), BF16),
            pltpu.VMEM((GRP, MAPR, 2 * DK), BF16),
            pltpu.VMEM((YN, MAPR, 2 * DK), BF16),
            pltpu.VMEM((GRP - 1, DK, 2 * DK), F32),
            pltpu.VMEM((GRP - 1, 1, 2 * DK), F32),
            pltpu.VMEM((DK, 2 * DK), F32),
            pltpu.VMEM((1, 2 * DK), F32),
            pltpu.VMEM((DK, DK), BF16),
            pltpu.VMEM((DK, DK), BF16),
            pltpu.VMEM((GRP, DK, DK), BF16),
            pltpu.VMEM((GRP, DK, DK), BF16),
            pltpu.VMEM((SPAN, QTR, 2 * QROWS, HA), BF16),
            pltpu.VMEM((2 * TOK, 1), F32),
            pltpu.VMEM((2 * TOK, 1), F32),
            pltpu.VMEM((2 * TOK, HA), F32),
            pltpu.VMEM((TOK, 4 * DK), BF16),
            pltpu.VMEM((TOK, 2 * HA), BF16),
            pltpu.VMEM((4, TOK, 256), BF16),
            pltpu.VMEM((4, TOK, 256), BF16),
            pltpu.VMEM((3, TOK, 256), BF16),
            pltpu.VMEM((3, TOK, 256), BF16),
            dma((9,)),
        ]
        + [dma((3,))] * 6
        + [dma((3,)), dma]
        + [dma((3,))] * 2
        + [dma((SPAN,))] * 2
        + [dma((SPAN, 3))] * 2
        + [dma((ZN // 2,))] * 4
        + [dma((3,))] * 2
        + [dma((4,))] * 2
        + [dma((3,))] * 2,
        compiler_params=pltpu.CompilerParams(
            vmem_limit_bytes=56 * MB, collective_id=1, has_side_effects=True
        ),
        name="mixer",
    )(
        weight_rows, delta_key, delta_query, delta_value, attn_key, attn_value, attn_query, output_gate, attn_gate,
        write_strength, log_decay, positions.reshape(1, TOK), block_lists, jnp.asarray(turn_table()), norm_gain.reshape(1, DK),
    )
    return (residual.astype(F32) + summed).astype(BF16)


def solution(mesh):
    return jax.shard_map(
        per_device,
        mesh=mesh,
        in_specs=(
            P("ctx", "mp"),
            P("ctx", "mp"),
            P("ctx", "mp"),
            P("ctx", "mp"),
            P("mp", "ctx"),
            P("mp", "ctx"),
            P("ctx", "mp"),
            P(),
            P("ctx", "mp"),
            P("ctx", None),
            P("ctx", None),
            P("ctx", "mp"),
            P("ctx"),
            P("ctx", None),
            P(None, "mp", "ctx"),
        ),
        out_specs=P("ctx", "mp"),
        check_vma=False,
    )
```
